256 devices in a mesh: grp: 8 (over x, core), tp: 32 (over y, z).
Axes of the slice: x: 4, y: 4, z: 8, core: 2. Of those that a mesh axis runs over, the one named last changes fastest.
Arguments:
- queries: bfloat16 [256, 8192], P('grp', 'tp'), may hold values from -12 to 12
- prefix_ids: int32 [256, 1], P('grp'), may hold values from 0 to 15; in each aligned block of 32 rows (0 to 31, 32 to 63, ...) at most 4 rows name the same one
- suffix_lengths: int32 [256], P('grp'), may hold values from 2 to 512
- owner_slots: int32 [16], replicated, may hold values from 0 to 15, each once
- prefix_cache: bfloat16 [2, 16, 8192, 1024], P(None, 'grp', 'tp'), may hold values from -5 to 5
- suffix_cache: bfloat16 [2, 256, 512, 1024], P(None, 'grp', 'tp'), may hold values from -5 to 5
- wo: bfloat16 [8192, 8192], P('tp'), may hold values from -0.0625 to 0.0625
Outputs:
- layer_out: bfloat16 [256, 8192], P('grp', 'tp')
The draws below stay inside these ranges and needn't reach their ends.
Inputs may be any that keep to these rules, and one draw needn't show every extreme that they name: `prefix_ids`: in the rows of one index of grp (aligned blocks of 32 requests) no prefix id appears more than 4 times. `owner_slots`: A permutation; slot j of prefix_cache lies on index j // 2 of grp.
All inputs are finite; a program needn't handle non-finite values.
Results may differ from the reference program's by a relative error of at most 0.024.
Values may be sent and summed in bfloat16 or wider, within the bound.
A program may use at most 128 MiB of HBM per device.

```python
import functools
import math
import jax
import jax.numpy as jnp
import numpy as np
from jax import lax

D = 8192
HQ = 64
KVH = 8
HD = 128
REQ_GRP = 32
PLEN_DEV = 256
SUF_DEV = 16
CAP = 4
REQUESTS = 256
PREFIXES = 16
PLEN = 8192
SUF = 512
N_TP = 32


def draw_queries(key, part):
    key = jax.random.fold_in(key, 1)
    drawn = jnp.clip(3.0 * jax.random.normal(key, (REQUESTS, HQ * HD), jnp.float32), -12.0, 12.0)
    return drawn.astype(jnp.bfloat16)


def draw_prefix_cache(key, part):
    key = jax.random.fold_in(key, 4)
    shape = (2, PREFIXES, PLEN, KVH * HD)
    drawn = jnp.clip(jax.random.normal(key, shape, jnp.float32), -5.0, 5.0)
    return drawn.astype(jnp.bfloat16)


def draw_suffix_cache(key, part):
    key = jax.random.fold_in(key, 2)
    drawn = jnp.clip(jax.random.normal(key, (2, REQUESTS, SUF, KVH * HD), jnp.float32), -5.0, 5.0)
    return drawn.astype(jnp.bfloat16)


def draw_suffix_lengths(key, part):
    key = jax.random.fold_in(key, 3)
    drawn = jax.random.randint(key, (REQUESTS,), 2, SUF + 1)
    indices = jnp.arange(REQUESTS)
    drawn = jnp.where(indices % 32 == 5, SUF, drawn)
    return drawn.astype(jnp.int32)


def shard_levels(own_key, extent, pieces, low, high):
    def one(dim, parts):
        steps = jax.random.uniform(jax.random.fold_in(jax.random.fold_in(own_key, 6), dim), (parts,), jnp.float32, low / len(pieces), high / len(pieces))
        return jnp.repeat(jnp.exp(steps), extent[dim] // parts).reshape((-1,) + (1,) * (len(extent) - dim - 1))

    loudness = one(*pieces[0])
    for cut in pieces[1:]:
        loudness = loudness * one(*cut)
    return loudness


def shared_out(rng, own, number, rows, number_of, top, most, slope):
    ranking = jax.random.permutation(rng, number_of)
    heavy_load, usual = portions_of(number_of, rows * top, most, slope, True), portions_of(number_of, rows * top, most, slope, False)
    places = jnp.arange(number_of)

    def named(lengths, offset_by):
        used = int((lengths > 0).sum())
        fixed = max(1, used // 4)
        passed = fixed + (places - fixed + offset_by * (used - fixed)) % max(1, number_of - fixed)
        return jnp.zeros((number_of,), jnp.int32).at[ranking[jnp.where(places < fixed, places, passed)]].set(jnp.asarray(lengths, jnp.int32))

    lengths = jnp.where(number % 4 == 0, named(heavy_load, number // 4), named(usual, number - number // 4 - 1))
    mixed = jax.random.permutation(jax.random.fold_in(own, 3), number_of)
    giver, receiver = mixed[0:number_of // 2 * 2:2], mixed[1:number_of // 2 * 2:2]
    room = jnp.minimum(lengths[giver] - 1, most - lengths[receiver]) // 2
    room = jnp.where((giver == ranking[0]) | (receiver == ranking[0]) | (lengths[receiver] == 0), 0, jnp.maximum(room, 0))
    passed = jax.random.randint(jax.random.fold_in(own, 4), (number_of // 2,), 0, 1 << 20) % (room + 1)
    lengths = lengths.at[giver].add(-passed).at[receiver].add(passed)
    members = jnp.searchsorted(jnp.cumsum(lengths), jnp.arange(rows * top), side="right").astype(jnp.int32)
    grid = members.reshape(top, rows).T
    grid = grid[jax.random.permutation(jax.random.fold_in(own, 1), rows)]
    offset_by = jax.random.randint(jax.random.fold_in(own, 2), (rows, 1), 0, top)
    return jnp.take_along_axis(grid, (jnp.arange(top)[None, :] + offset_by) % top, axis=1)


def portions_of(amount, total, most, slope, full):
    loads = [(1 << 20) // math.isqrt(rank ** slope) + 1 for rank in range(1, amount + 1)]
    largest = most if full else min(most, max(-(-total // amount), total * loads[0] // sum(loads)))
    least = 1 if total - largest >= amount - 1 else 0
    given, surplus = [largest] + [least] * (amount - 1), total - largest - least * (amount - 1)
    while surplus > 0:
        free = [i for i in range(1, amount) if given[i] < largest] or [i for i in range(1, amount) if given[i] < most]
        whole, left = sum([loads[i] for i in free]), surplus
        for i in free:
            more = min(most - given[i], max(1, left * loads[i] // whole), surplus)
            given[i] = given[i] + more
            surplus = surplus - more
    return np.array(given)


def normal_values(own_key, extent, scale, reach, split=(), kind=jnp.bfloat16):
    values = scale * jax.random.normal(own_key, extent, jnp.float32)
    if split:
        values = values * shard_levels(own_key, extent, split, -0.22, 0.18)
    return jnp.clip(values, -reach, reach).astype(kind)


def setup_inputs(seed: int = 0) -> dict:
    key_list = jax.random.split(jax.random.key(seed), 8)
    queries = draw_queries(jax.random.fold_in(key_list[7], 71), 0)
    prefix_ids_keys = jax.random.split(jax.random.fold_in(key_list[1], 1), REQUESTS // REQ_GRP)
    prefix_ids_turns = jax.random.permutation(jax.random.fold_in(key_list[1], 3), REQUESTS // REQ_GRP)
    prefix_ids = jax.vmap(lambda own, number: shared_out(jax.random.fold_in(key_list[1], 2), own, number, REQ_GRP, PREFIXES, 1, CAP, 2))(prefix_ids_keys, prefix_ids_turns).reshape((REQUESTS, 1))
    suffix_lengths = draw_suffix_lengths(jax.random.fold_in(key_list[7], 71), 0)
    owner_slots = jax.random.permutation(key_list[3], PREFIXES).astype(jnp.int32)
    prefix_cache = draw_prefix_cache(jax.random.fold_in(key_list[7], 71), 0)
    suffix_cache = draw_suffix_cache(jax.random.fold_in(key_list[7], 71), 0)
    wo = normal_values(key_list[6], (HQ * HD, D), (HQ * HD) ** -0.5, 0.0625, ((0, 32),))
    return {"queries": queries, "prefix_ids": prefix_ids, "suffix_lengths": suffix_lengths, "owner_slots": owner_slots, "prefix_cache": prefix_cache, "suffix_cache": suffix_cache, "wo": wo}


negative_fill = -1e+30

def block_stats(scores, usable):
    scores = jnp.where(usable, scores, negative_fill)
    highest = lax.optimization_barrier(jnp.max(scores, axis=-1))
    weights = jnp.where(usable, jnp.exp(scores - highest[..., None]), 0.0).astype(jnp.bfloat16)
    totals = lax.optimization_barrier(jnp.sum(weights.astype(jnp.float32), axis=-1))
    return (highest, weights, totals)

def one_request(inputs, prefix_cache):
    query_row, slot_of, suffix_keys, suffix_values, length = inputs
    group_size = HQ // KVH
    score_scale = 1.0 / math.sqrt(HD)
    asking = query_row.astype(jnp.float32).reshape(KVH, group_size, HD)
    chosen = lax.dynamic_index_in_dim(prefix_cache, slot_of.astype(jnp.int32), axis=1, keepdims=False)
    chosen = chosen.astype(jnp.float32).reshape(2, N_TP, PLEN_DEV, KVH, HD)
    pre_scores = jnp.einsum('kgd,ntkd->nkgt', asking, chosen[0]) * score_scale
    pre_high, pre_weights, pre_totals = block_stats(pre_scores, True)
    pre_sums = jnp.einsum('nkgt,ntkd->nkgd', pre_weights.astype(jnp.float32), chosen[1])
    suf_keys = suffix_keys.astype(jnp.float32).reshape(N_TP, SUF_DEV, KVH, HD)
    suf_values = suffix_values.astype(jnp.float32).reshape(N_TP, SUF_DEV, KVH, HD)
    positions = jnp.arange(N_TP * SUF_DEV, dtype=jnp.int32).reshape(N_TP, SUF_DEV)
    usable = (positions < length.astype(jnp.int32))[:, None, None, :]
    suf_scores = jnp.einsum('kgd,ntkd->nkgt', asking, suf_keys) * score_scale
    suf_high, suf_weights, suf_totals = block_stats(suf_scores, usable)
    suf_sums = jnp.einsum('nkgt,ntkd->nkgd', suf_weights.astype(jnp.float32), suf_values)
    highest = jnp.concatenate([pre_high, suf_high], axis=0)
    totals = jnp.concatenate([pre_totals, suf_totals], axis=0)
    summed = jnp.concatenate([pre_sums, suf_sums], axis=0)
    largest = lax.optimization_barrier(jnp.max(highest, axis=0))
    factor = jnp.exp(highest - largest)
    numer = lax.optimization_barrier(jnp.sum(summed * factor[..., None], axis=0))
    denom = lax.optimization_barrier(jnp.sum(totals * factor, axis=0))
    return (numer / denom[..., None]).astype(jnp.bfloat16).reshape(HQ * HD)

def reference(queries, prefix_ids, suffix_lengths, owner_slots, prefix_cache, suffix_cache, wo):
    slot_of = owner_slots[prefix_ids[:, 0]].astype(jnp.int32)
    attended = lax.map(functools.partial(one_request, prefix_cache=prefix_cache), (queries, slot_of, suffix_cache[0], suffix_cache[1], suffix_lengths))
    return jnp.dot(attended, wo, preferred_element_type=jnp.float32).astype(jnp.bfloat16)
```

```python
import functools
import math

import jax
import jax.numpy as jnp
from jax import lax
from jax.experimental import pallas as pl
from jax.experimental.pallas import tpu as pltpu
from jax.sharding import PartitionSpec as P

HD = 128
OWN = 2
SLOTS = 2
CAP = 4
LANES = SLOTS * CAP
Z_SIZE = 8
MASKED = -1e30
MESH = pl.DeviceIdType.MESH


def nt(a, b):
    return lax.dot_general(a, b, (((1,), (1,)), ((), ())), preferred_element_type=jnp.float32)


def mm(a, b):
    return jnp.dot(a, b, preferred_element_type=jnp.float32)


def iota(shape, dim):
    return lax.broadcasted_iota(jnp.int32, shape, dim)


def diagonal(rows, shift=0):
    return iota((rows, 128), 1) == iota((rows, 128), 0) + shift


def to_row(column, rows):
    wide = jnp.broadcast_to(column, (rows, 128))
    return jnp.sum(jnp.where(diagonal(rows), wide, 0.0), axis=0, keepdims=True)


def to_column(row, rows, shift=0):
    wide = jnp.broadcast_to(row, (rows, 128))
    return jnp.sum(jnp.where(diagonal(rows, shift), wide, 0.0), axis=1, keepdims=True)


def merge(parts):
    largest = functools.reduce(jnp.maximum, [level for _, level in parts])
    factors = [jnp.exp(level - largest) for _, level in parts]
    total = functools.reduce(jnp.add, factors)
    summed = functools.reduce(jnp.add, [f * value for f, (value, _) in zip(factors, parts)])
    return summed / total, largest + jnp.log(total)


def attend(scores, values):
    highest = jnp.max(scores, axis=1, keepdims=True)
    weights = jnp.exp(scores - highest)
    totals = jnp.sum(weights, axis=1, keepdims=True)
    summed = mm(weights.astype(jnp.bfloat16), values)
    return summed / totals, highest + jnp.log(totals)


def kernel(
    dims,
    q_ref, crow_ref, ccol_ref, pc_ref, sc_ref, wo_ref, out_ref,
    pk, sk, wv, qall, xs, xr, po, pr, ls, lr, lc, so, sl, sel, back, gsel, lsel, bias,
    yb, yl, yr, ylr, zb, zl, zr, zlr, wp, wr, wz, wzr,
    in_sem, a_send, a_recv, b_send, b_recv, c_send, c_recv, e_send, e_recv, el_send, el_recv,
    y_send, y_recv, yl_send, yl_recv, z_send, z_recv, zl_send, zl_recv,
    wy_send, wy_recv, wz_send, wz_recv, own_sem,
):
    groups, ys, zs, kvh, rows, suf = dims
    ky = kvh // ys
    dk = ys * zs // kvh
    size = dk * OWN
    n = size * rows
    strip = SLOTS * size * CAP
    lane_rows = ky * strip
    small = size * CAP
    scale = 1.0 / math.sqrt(HD)
    grp = lax.axis_index("grp")
    tp = lax.axis_index("tp")
    y = tp // zs
    z = tp % zs

    def remote(src, dst, send, recv, device):
        return pltpu.make_async_remote_copy(
            src_ref=src, dst_ref=dst, send_sem=send, recv_sem=recv,
            device_id=device, device_id_type=MESH,
        )

    def each(low, high, fn):
        def step(i, c):
            fn(i)
            return c
        lax.fori_loop(low, high, step, 0)

    loads = [
        pltpu.make_async_copy(pc_ref, pk, in_sem.at[0]),
        pltpu.make_async_copy(sc_ref, sk, in_sem.at[1]),
        pltpu.make_async_copy(wo_ref, wv, in_sem.at[2]),
    ]
    for load in loads:
        load.start()

    def z_peer(d):
        return (grp, y * zs + (z + d) % zs)

    def y_peer(d):
        return (grp, ((y + d) % ys) * zs + z)

    def y_back(d):
        return (grp, ((y - d + ys) % ys) * zs + z)

    def g_peer(d):
        return ((grp + d) % groups, tp)

    barrier = pltpu.get_barrier_semaphore()
    each(1, zs, lambda d: pl.semaphore_signal(barrier, inc=1, device_id=z_peer(d), device_id_type=MESH))
    each(1, ys, lambda d: pl.semaphore_signal(barrier, inc=1, device_id=y_peer(d), device_id_type=MESH))
    each(1, groups, lambda d: pl.semaphore_signal(barrier, inc=1, device_id=g_peer(d), device_id_type=MESH))

    qall[tp, 0:rows, :] = q_ref[:, 0:HD]
    qall[tp, rows : 2 * rows, :] = q_ref[:, HD : 2 * HD]
    pl.semaphore_wait(barrier, zs + ys + groups - 3)

    def a_copy(d):
        return remote(qall.at[tp], qall.at[tp], a_send.at[d], a_recv.at[d], z_peer(d))

    each(1, zs, lambda d: a_copy(d).start())

    code = ccol_ref[...] % 512
    length = ccol_ref[...] // 512
    target = code % (groups * LANES)
    head = code // (groups * LANES)
    gsel[...] = target // LANES
    lsel[...] = ((target // CAP) % SLOTS) * small + head * CAP + target % CAP
    wide = groups * strip

    def lane_code(i):
        return (i // strip) * LANES + ((i // small) % SLOTS) * CAP + i % CAP + groups * LANES * ((i // CAP) % size)

    sel[...] = jnp.where(
        lane_code(iota((wide, n), 0)) == crow_ref[0:1, :] % 512, 1.0, 0.0
    ).astype(jnp.bfloat16)
    back[...] = jnp.where(
        lane_code(iota((n, wide), 1)) == code[:, 0:1], 1.0, 0.0
    ).astype(jnp.bfloat16)
    position = iota((n, rows * suf), 1)
    kept = (position // suf == iota((n, rows * suf), 0) % rows) & (
        position % suf + tp * suf < length[:, 0:1]
    )
    bias[...] = jnp.where(kept, 0.0, MASKED)

    each(1, zs, lambda d: a_copy(d).wait_recv())

    def b_copy(d):
        return remote(
            qall.at[pl.ds(y * zs, zs)], qall.at[pl.ds(y * zs, zs)],
            b_send.at[d], b_recv.at[d], y_peer(d),
        )

    each(1, ys, lambda d: b_copy(d).start())

    def block_of(d):
        return (y - d + ys) % ys

    def c_copy(d, e):
        yy = block_of(d)
        return remote(
            xs.at[yy, (grp + e) % groups], xr.at[yy, grp],
            c_send.at[d, e], c_recv.at[d, e], g_peer(e),
        )

    def own_copy(d):
        yy = block_of(d)
        return pltpu.make_async_copy(xs.at[yy, grp], xr.at[yy, grp], own_sem.at[0, d])

    def c_stage(d):
        yy = block_of(d)
        for kk in range(ky):
            block = qall[pl.ds((yy * ky + kk) * dk, dk)].reshape(n, HD)
            picked = mm(sel[...], block).astype(jnp.bfloat16)
            xs[yy, :, kk * strip : (kk + 1) * strip, :] = picked.reshape(groups, strip, HD)
        own_copy(d).start()
        each(1, groups, lambda e: c_copy(d, e).start())

    c_stage(0)

    def b_step(d):
        b_copy(d).wait_recv()
        c_stage(d)

    each(1, ys, b_step)

    loads[1].wait()

    def suffix(k):
        lanes = pl.ds(pl.multiple_of(k * HD, HD), HD)
        block = qall[pl.ds(k * dk, dk)].reshape(n, HD)
        scores = nt(block, sk[0, :, lanes]) * scale + bias[...]
        value, level = attend(scores, sk[1, :, lanes])
        so[k] = value
        sl[k] = jnp.broadcast_to(level, (n, 128))

    each(0, kvh, suffix)

    loads[0].wait()

    def e_copy(d, e):
        yy = block_of(d)
        return remote(
            po.at[yy, (grp + e) % groups], pr.at[yy, grp],
            e_send.at[d, e], e_recv.at[d, e], g_peer(e),
        )

    def el_copy(d, e):
        yy = block_of(d)
        return remote(
            ls.at[yy, (grp + e) % groups], lr.at[yy, grp],
            el_send.at[d, e], el_recv.at[d, e], g_peer(e),
        )

    def own_back(d):
        yy = block_of(d)
        return pltpu.make_async_copy(po.at[yy, grp], pr.at[yy, grp], own_sem.at[1, d])

    def own_level(d):
        yy = block_of(d)
        return pltpu.make_async_copy(ls.at[yy, grp], lr.at[yy, grp], own_sem.at[2, d])

    def prefix(d):
        yy = block_of(d)
        own_copy(d).wait()
        each(1, groups, lambda e: c_copy(d, e).wait_recv())
        for kk in range(ky):
            lanes = pl.ds(pl.multiple_of((yy * ky + kk) * HD, HD), HD)
            for j in range(SLOTS):
                part = slice(kk * strip + j * small, kk * strip + (j + 1) * small)
                asking = xr[yy, :, part, :].reshape(groups * small, HD)
                scores = nt(asking, pk[0, j, :, lanes]) * scale
                value, level = attend(scores, pk[1, j, :, lanes])
                po[yy, :, part, :] = value.astype(jnp.bfloat16).reshape(groups, small, HD)
                lc[:, part, :] = jnp.broadcast_to(level, (groups * small, 128)).reshape(
                    groups, small, 128
                )

        def pack(g):
            ls[yy, g] = jnp.broadcast_to(to_row(lc[g], lane_rows), (8, 128))

        each(0, groups, pack)
        own_back(d).start()
        own_level(d).start()

        def send(e):
            e_copy(d, e).start()
            el_copy(d, e).start()

        each(1, groups, send)

    each(0, ys, prefix)

    def y_copy(d):
        return remote(yb.at[block_of(d)], yr.at[d], y_send.at[d], y_recv.at[d], y_back(d))

    def yl_copy(d):
        return remote(yl.at[block_of(d)], ylr.at[d], yl_send.at[d], yl_recv.at[d], y_back(d))

    def join(d):
        yy = block_of(d)
        own_back(d).wait()
        own_level(d).wait()

        def arrived(e):
            e_copy(d, e).wait_recv()
            el_copy(d, e).wait_recv()

        each(1, groups, arrived)
        levels = jnp.zeros((n, 128), jnp.float32)
        for g in range(groups):
            levels = jnp.where(gsel[...] == g, lr[yy, g, 0:1, :], levels)
        for kk in range(ky):
            hit = iota((n, 128), 1) == lsel[...] + kk * strip
            level = jnp.sum(jnp.where(hit, levels, 0.0), axis=1, keepdims=True)
            parts = pr[yy, :, kk * strip : (kk + 1) * strip, :].reshape(wide, HD)
            k = yy * ky + kk
            value, joint = merge([(mm(back[...], parts), level), (so[k], sl[k][:, 0:1])])
            yb[yy, kk * n : (kk + 1) * n, :] = value.astype(jnp.bfloat16)
            for i in range(n // 128):
                at = kk * (n // 128) + i
                yl[yy, at : at + 1, :] = to_row(joint[i * 128 : (i + 1) * 128], 128)

    join(0)

    def y_step(d):
        join(d)
        y_copy(d).start()
        yl_copy(d).start()

    each(1, ys, y_step)

    def y_arrived(d):
        y_copy(d).wait_recv()
        yl_copy(d).wait_recv()

    each(1, ys, y_arrived)

    def y_merge(i):
        rows_at = pl.ds(pl.multiple_of(i * 128, 128), 128)
        parts = [(yb[y, rows_at, :].astype(jnp.float32), to_column(yl[y, pl.ds(i, 1), :], 128))]
        for d in range(1, ys):
            parts.append(
                (yr[d, rows_at, :].astype(jnp.float32), to_column(ylr[d, pl.ds(i, 1), :], 128))
            )
        value, level = merge(parts)
        zb[pl.ds(i * 2, 2)] = value.astype(jnp.bfloat16).reshape(2, 64, HD)
        zl[pl.ds(i * 2, 2)] = jnp.broadcast_to(to_row(level, 128)[None], (2, 8, 128))

    each(0, zs // 2, y_merge)

    def z_copy(d):
        return remote(zb.at[(z + d) % zs], zr.at[d], z_send.at[d], z_recv.at[d], z_peer(d))

    def zl_copy(d):
        return remote(zl.at[(z + d) % zs], zlr.at[d], zl_send.at[d], zl_recv.at[d], z_peer(d))

    def z_start(d):
        z_copy(d).start()
        zl_copy(d).start()

    each(1, zs, z_start)

    def z_arrived(d):
        z_copy(d).wait_recv()
        zl_copy(d).wait_recv()

    each(1, zs, z_arrived)
    shift = (z % 2) * 64
    parts = [(zb[z].astype(jnp.float32), to_column(zl[z, 0:1, :], 64, shift))]
    for d in range(1, zs):
        parts.append((zr[d].astype(jnp.float32), to_column(zlr[d, 0:1, :], 64, shift)))
    attended = merge(parts)[0].astype(jnp.bfloat16)

    loads[2].wait()

    def wy_copy(d):
        return remote(wp.at[block_of(d)], wr.at[d], wy_send.at[d], wy_recv.at[d], y_back(d))

    def project(d):
        yy = block_of(d)

        def piece(i):
            columns = pl.ds(pl.multiple_of((yy * zs + i) * OWN * HD, OWN * HD), OWN * HD)
            total = mm(attended[0:rows], wv[0:HD, columns])
            total += mm(attended[rows : 2 * rows], wv[HD : 2 * HD, columns])
            wp[yy, i] = total.astype(jnp.bfloat16)

        each(0, zs, piece)

    def project_step(d):
        project(d)
        wy_copy(d).start()

    each(1, ys, project_step)
    project(0)
    each(1, ys, lambda d: wy_copy(d).wait_recv())

    def w_sum(i):
        total = wp[y, i].astype(jnp.float32)
        for d in range(1, ys):
            total += wr[d, i].astype(jnp.float32)
        wz[i] = total.astype(jnp.bfloat16)

    each(0, zs, w_sum)

    def wz_copy(d):
        return remote(wz.at[(z + d) % zs], wzr.at[d], wz_send.at[d], wz_recv.at[d], z_peer(d))

    each(1, zs, lambda d: wz_copy(d).start())
    each(1, zs, lambda d: wz_copy(d).wait_recv())
    total = wz[z].astype(jnp.float32)
    for d in range(1, zs):
        total += wzr[d].astype(jnp.float32)
    out_ref[...] = total.astype(jnp.bfloat16)

    def z_sent(d):
        a_copy(d).wait_send()
        z_copy(d).wait_send()
        zl_copy(d).wait_send()
        wz_copy(d).wait_send()

    each(1, zs, z_sent)

    def y_sent(d):
        b_copy(d).wait_send()
        y_copy(d).wait_send()
        yl_copy(d).wait_send()
        wy_copy(d).wait_send()

    each(1, ys, y_sent)

    def g_sent(d):
        def one(e):
            c_copy(d, e).wait_send()
            e_copy(d, e).wait_send()
            el_copy(d, e).wait_send()

        each(1, groups, one)

    each(0, ys, g_sent)


def body(zs, queries, prefix_ids, suffix_lengths, owner_slots, prefix_cache, suffix_cache, wo):
    groups = lax.axis_size("grp")
    shards = lax.axis_size("tp")
    ys = shards // zs
    rows = queries.shape[0]
    suf = suffix_cache.shape[2]
    kvh = prefix_cache.shape[3] // HD
    size = shards * OWN // kvh
    n = size * rows
    ky = kvh // ys
    strip = SLOTS * size * CAP
    lane_rows = ky * strip

    ids = prefix_ids[:, 0]
    slots = jnp.arange(owner_slots.shape[0])
    slot_of = jnp.sum(jnp.where(ids[:, None] == slots[None, :], owner_slots[None, :], 0), axis=1)
    order = jnp.arange(rows)
    earlier = (ids[:, None] == ids[None, :]) & (order[:, None] > order[None, :])
    target = slot_of * CAP + jnp.sum(earlier.astype(jnp.int32), axis=1)
    base = target + 512 * suffix_lengths
    heads = jnp.arange(size, dtype=jnp.int32) * (groups * LANES)
    code = (heads[:, None] + base[None, :]).reshape(n)
    code_row = jnp.broadcast_to(code[None, :], (8, n))
    code_col = jnp.broadcast_to(code[:, None], (n, 128))

    dims = (groups, ys, zs, kvh, rows, suf)
    bf, f32 = jnp.bfloat16, jnp.float32
    dma = pltpu.SemaphoreType.DMA
    vmem = pl.BlockSpec(memory_space=pltpu.VMEM)
    hbm = pl.BlockSpec(memory_space=pl.ANY)
    V = pltpu.VMEM
    scratch = [
        V(prefix_cache.shape, bf),
        V((2, rows * suf, kvh * HD), bf),
        V(wo.shape, bf),
        V((shards, OWN * rows, HD), bf),
        V((ys, groups, lane_rows, HD), bf),
        V((ys, groups, lane_rows, HD), bf),
        V((ys, groups, lane_rows, HD), bf),
        V((ys, groups, lane_rows, HD), bf),
        V((ys, groups, 8, 128), f32),
        V((ys, groups, 8, 128), f32),
        V((groups, lane_rows, 128), f32),
        V((kvh, n, HD), f32),
        V((kvh, n, 128), f32),
        V((groups * strip, n), bf),
        V((n, groups * strip), bf),
        V((n, 128), jnp.int32),
        V((n, 128), jnp.int32),
        V((n, rows * suf), f32),
        V((ys, ky * n, HD), bf),
        V((ys, 8, 128), f32),
        V((ys, ky * n, HD), bf),
        V((ys, 8, 128), f32),
        V((zs, OWN * rows, HD), bf),
        V((zs, 8, 128), f32),
        V((zs, OWN * rows, HD), bf),
        V((zs, 8, 128), f32),
        V((ys, zs, rows, OWN * HD), bf),
        V((ys, zs, rows, OWN * HD), bf),
        V((zs, rows, OWN * HD), bf),
        V((zs, rows, OWN * HD), bf),
        dma((3,)),
        dma((zs,)), dma((zs,)),
        dma((ys,)), dma((ys,)),
        dma((ys, groups)), dma((ys, groups)),
        dma((ys, groups)), dma((ys, groups)),
        dma((ys, groups)), dma((ys, groups)),
        dma((ys,)), dma((ys,)), dma((ys,)), dma((ys,)),
        dma((zs,)), dma((zs,)), dma((zs,)), dma((zs,)),
        dma((ys,)), dma((ys,)),
        dma((zs,)), dma((zs,)),
        dma((3, ys)),
    ]
    return pl.pallas_call(
        functools.partial(kernel, dims),
        out_shape=jax.ShapeDtypeStruct((rows, wo.shape[1] // shards), bf),
        in_specs=[vmem, vmem, vmem, hbm, hbm, hbm],
        out_specs=vmem,
        scratch_shapes=scratch,
        compiler_params=pltpu.CompilerParams(
            collective_id=0, has_side_effects=True, vmem_limit_bytes=48 * 1024 * 1024
        ),
        name="decode_attention",
    )(
        queries, code_row, code_col, prefix_cache,
        suffix_cache.reshape(2, rows * suf, kvh * HD), wo,
    )


def solution(mesh, zs=Z_SIZE):
    placed = (
        P("grp", "tp"),
        P("grp", None),
        P("grp"),
        P(),
        P(None, "grp", "tp", None),
        P(None, "grp", "tp", None),
        P("tp", None),
    )
    return jax.shard_map(
        functools.partial(body, zs),
        mesh=mesh, in_specs=placed, out_specs=P("grp", "tp"), check_vma=False,
    )
```

```python
import functools
import math

import jax
import jax.numpy as jnp
from jax import lax
from jax.experimental import pallas as pl
from jax.experimental.pallas import tpu as pltpu
from jax.sharding import PartitionSpec as P

HD = 128
OWN = 2
SLOTS = 2
CAP = 4
LANES = SLOTS * CAP
Z_SIZE = 8
NEAR = 6
MASKED = -1e30
MESH = pl.DeviceIdType.MESH


def div(a, b):
    return a // b if isinstance(a, int) else lax.div(a, jnp.full_like(a, b))


def rem(a, b):
    return a % b if isinstance(a, int) else lax.rem(a, jnp.full_like(a, b))


def turn(i):
    return i + div(i, 2) * (1 - 2 * rem(i, 2))


def outward(i, count):
    return count // 2 + (1 - 2 * rem(i, 2)) * div(i + 1, 2)


def nt(a, b):
    return lax.dot_general(a, b, (((1,), (1,)), ((), ())), preferred_element_type=jnp.float32)


def mm(a, b):
    return jnp.dot(a, b, preferred_element_type=jnp.float32)


def iota(shape, dim):
    return lax.broadcasted_iota(jnp.int32, shape, dim)


def diagonal(rows, shift=0):
    return iota((rows, 128), 1) == iota((rows, 128), 0) + shift


def to_row(column, rows):
    wide = jnp.broadcast_to(column, (rows, 128))
    return jnp.sum(jnp.where(diagonal(rows), wide, 0.0), axis=0, keepdims=True)


def to_column(row, rows, shift=0):
    wide = jnp.broadcast_to(row, (rows, 128))
    return jnp.sum(jnp.where(diagonal(rows, shift), wide, 0.0), axis=1, keepdims=True)


def merge(parts):
    largest = functools.reduce(jnp.maximum, [level for _, level in parts])
    factors = [jnp.exp(level - largest) for _, level in parts]
    total = functools.reduce(jnp.add, factors)
    summed = functools.reduce(jnp.add, [f * value for f, (value, _) in zip(factors, parts)])
    return summed / total, largest + jnp.log(total)


def spread(row, shape, index):
    return jnp.sum(jnp.where(iota(shape, 1) == index, row, 0.0), axis=1, keepdims=True)


def attend(products, values):
    scale = 1.0 / math.sqrt(HD)
    highest = jnp.max(products, axis=1, keepdims=True)
    weights = jnp.exp((products - highest) * scale)
    totals = jnp.sum(weights, axis=1, keepdims=True)
    summed = mm(weights.astype(jnp.bfloat16), values)
    return summed / totals, highest * scale + jnp.log(totals)


def kernel(
    dims,
    q_ref, ids_ref, len_ref, slots_ref, pc_ref, sc_ref, wo_ref, out_ref,
    qv, idv, lenv, slotv, pk, sk, wv, qall, xs, xr, po, pr, ls, lr, fr, flr, fo, fl, lc, so, sl, sel, back, gsel, lsel, bias,
    yb, yl, yr, ylr, zb, zl, zr, zlr, wp, wr, wz, wzr,
    in_sem, a_send, a_recv, b_send, b_recv, c_send, c_recv, f_send, f_recv,
    e_send, e_recv, el_send, el_recv, r_send, r_recv, rl_send, rl_recv, m_send, m_recv, ml_send, ml_recv,
    y_send, y_recv, yl_send, yl_recv, z_send, z_recv, zl_send, zl_recv,
    wy_send, wy_recv, wz_send, wz_recv,
):
    groups, ys, zs, kvh, rows, suf = dims
    ky = kvh // ys
    dk = ys * zs // kvh
    size = dk * OWN
    n = size * rows
    strip = SLOTS * size * CAP
    lane_rows = ky * strip
    small = size * CAP
    half = rows // 2
    grp = lax.axis_index("grp")
    tp = lax.axis_index("tp")
    y = div(tp, zs)
    z = rem(tp, zs)

    def remote(src, dst, send, recv, device):
        return pltpu.make_async_remote_copy(
            src_ref=src, dst_ref=dst, send_sem=send, recv_sem=recv,
            device_id=device, device_id_type=MESH,
        )

    def each(low, high, fn):
        def step(i, c):
            fn(i)
            return c
        lax.fori_loop(low, high, step, 0)

    loads = [
        pltpu.make_async_copy(q_ref, qv, in_sem.at[0]),
        pltpu.make_async_copy(ids_ref, idv, in_sem.at[1]),
        pltpu.make_async_copy(len_ref, lenv, in_sem.at[2]),
        pltpu.make_async_copy(slots_ref, slotv, in_sem.at[3]),
        pltpu.make_async_copy(sc_ref, sk, in_sem.at[4]),
        pltpu.make_async_copy(pc_ref, pk, in_sem.at[5]),
        pltpu.make_async_copy(wo_ref, wv, in_sem.at[6]),
    ]
    for load in loads:
        load.start()

    def z_peer(d):
        return (grp, y * zs + rem(z + d, zs))

    def y_peer(d):
        return (grp, rem(y + d, ys) * zs + z)

    def y_back(d):
        return (grp, rem(y - d + ys, ys) * zs + z)

    def owner(e):
        x, core = rem(div(grp, 2) + turn(div(e, 2)), groups // 2), rem(grp + e, 2)
        return x * 2 + core

    def asker(e):
        x, core = rem(div(grp, 2) + groups // 2 - turn(div(e, 2)), groups // 2), rem(grp + e, 2)
        return x * 2 + core

    barrier = pltpu.get_barrier_semaphore()
    each(1, zs, lambda d: pl.semaphore_signal(barrier, inc=1, device_id=z_peer(d), device_id_type=MESH))
    each(1, ys, lambda d: pl.semaphore_signal(barrier, inc=1, device_id=y_peer(d), device_id_type=MESH))
    each(1, groups, lambda d: pl.semaphore_signal(barrier, inc=1, device_id=(owner(d), tp), device_id_type=MESH))

    loads[0].wait()
    qall[tp, 0:rows, :] = qv[:, 0:HD]
    qall[tp, rows : 2 * rows, :] = qv[:, HD : 2 * HD]
    pl.semaphore_wait(barrier, zs + ys + groups - 3)

    def a_copy(d):
        return remote(qall.at[tp], qall.at[tp], a_send.at[d], a_recv.at[d], z_peer(d))

    def b_copy(i, d):
        piece = qall.at[y * zs + rem(z - i + zs, zs)]
        return remote(piece, piece, b_send.at[i, d], b_recv.at[i, d], y_peer(d))

    def forward(i):
        each(1, ys, lambda d: b_copy(i, d).start())

    each(0, zs - 1, lambda i: a_copy(outward(i, zs)).start())
    forward(0)

    for load in loads[1:4]:
        load.wait()
    ids = idv[...].astype(jnp.float32)
    lengths = lenv[...].astype(jnp.float32)
    slot_count = slotv.shape[1]
    slots = spread(slotv[...].astype(jnp.float32), (slot_count,) * 2, iota((slot_count,) * 2, 0))
    square = (rows, rows)
    ids_column = spread(ids, square, iota(square, 0))
    slot_of = jnp.sum(
        jnp.where(iota((slot_count, rows), 0).astype(jnp.float32) == ids, slots, 0.0),
        axis=0, keepdims=True,
    )
    earlier = (ids_column == ids) & (iota(square, 0) < iota(square, 1))
    target = slot_of * CAP + jnp.sum(jnp.where(earlier, 1.0, 0.0), axis=0, keepdims=True)
    target_column = spread(target, square, iota(square, 0))
    all_rows = jnp.sum(
        jnp.where(iota((rows, n), 0) == rem(iota((rows, n), 1), rows), target_column, 0.0),
        axis=0, keepdims=True,
    ).astype(jnp.int32) + (groups * LANES) * (div(iota((1, n), 1), rows))
    all_column = spread(target, (n, rows), rem(iota((n, rows), 0), rows)).astype(jnp.int32)
    head = div(iota((n, 128), 0), rows)
    place = jnp.broadcast_to(all_column, (n, 128))
    gsel[...] = div(place, LANES)
    lsel[...] = rem(div(place, CAP), SLOTS) * small + head * CAP + rem(place, CAP)
    wide = groups * strip

    def lane_code(i):
        lane = rem(div(i, small), SLOTS) * CAP + rem(i, CAP)
        return owner(div(i, strip)) * LANES + lane + groups * LANES * rem(div(i, CAP), size)

    sel[...] = jnp.where(lane_code(iota((wide, n), 0)) == all_rows, 1.0, 0.0).astype(jnp.bfloat16)
    back[...] = jnp.where(
        lane_code(iota((n, wide), 1)) == all_column + (groups * LANES) * div(iota((n, 1), 0), rows),
        1.0, 0.0,
    ).astype(jnp.bfloat16)
    box = (size * half, half * suf)
    for h in range(2):
        limit = spread(lengths, (size * half, rows), rem(iota((size * half, rows), 0), half) + h * half)
        kept = (div(iota(box, 1), suf) == rem(iota(box, 0), half)) & (
            rem(iota(box, 1), suf) + tp * suf < limit.astype(jnp.int32)
        )
        bias[h] = jnp.where(kept, 0.0, MASKED)

    def relay(i):
        d = outward(zs - 2 - i, zs)
        a_copy(d).wait_recv()
        forward(d)

    each(0, zs - 1, relay)

    def block_of(d):
        return rem(y - d + ys, ys)

    def c_copy(d, e):
        yy = block_of(d)
        return remote(
            xs.at[yy, e], xr.at[yy, e], c_send.at[d, e], c_recv.at[d, e], (owner(e), tp)
        )

    def c_stage(d):
        yy = block_of(d)
        for kk in range(ky):
            part = slice(kk * strip, (kk + 1) * strip)
            block = qall[pl.ds((yy * ky + kk) * dk, dk)].reshape(n, HD)
            picked = mm(sel[...], block).astype(jnp.bfloat16).reshape(groups, strip, HD)
            xs[yy, :, part, :] = picked
            xr[yy, 0, part, :] = picked[0]

    def f_copy(e, d):
        return remote(
            xr.at[y, e], xr.at[y, e], f_send.at[e - NEAR, d], f_recv.at[e - NEAR, d], y_peer(d)
        )

    def suffix(k):
        lanes = pl.ds(pl.multiple_of(k * HD, HD), HD)
        block = qall[pl.ds(k * dk, dk)].reshape(size, rows, HD)
        for h in range(2):
            part = slice(h * half, (h + 1) * half)
            at = slice(h * half * suf, (h + 1) * half * suf)
            asking = block[:, part, :].reshape(size * half, HD)
            value, level = attend(nt(asking, sk[0, at, lanes]) + bias[h], sk[1, at, lanes])
            so[k, :, part, :] = value.reshape(size, half, HD)
            sl[k, :, part, :] = jnp.broadcast_to(level, (size * half, 128)).reshape(size, half, 128)

    def suffixes(d):
        yy = block_of(d)
        for kk in range(ky):
            suffix(yy * ky + kk)

    c_stage(0)
    each(1, groups, lambda e: c_copy(0, groups - e).start())
    loads[4].wait()
    suffixes(0)

    def ask(i):
        d = turn(i)
        each(0, zs, lambda j: b_copy(j, d).wait_recv())
        c_stage(d)
        each(1, NEAR, lambda e: c_copy(d, e).start())
        suffixes(d)

    def pass_on(e):
        c_copy(0, e).wait_recv()
        each(1, ys, lambda d: f_copy(e, d).start())

    ask(1)
    each(NEAR, groups, pass_on)

    loads[5].wait()

    def e_copy(d, e):
        yy = block_of(d)
        return remote(
            po.at[yy, e], pr.at[yy, e], e_send.at[d, e], e_recv.at[d, e], (asker(e), tp)
        )

    def el_copy(d, e):
        yy = block_of(d)
        return remote(
            ls.at[yy, e], lr.at[yy, e], el_send.at[d, e], el_recv.at[d, e], (asker(e), tp)
        )

    def r_copy(e, d):
        i = e - NEAR
        return remote(
            po.at[block_of(d), e], fr.at[d, i], r_send.at[i, d], r_recv.at[i, d], y_back(d)
        )

    def rl_copy(e, d):
        i = e - NEAR
        return remote(
            ls.at[block_of(d), e], flr.at[d, i], rl_send.at[i, d], rl_recv.at[i, d], y_back(d)
        )

    def m_copy(e):
        i = e - NEAR
        return remote(fo.at[i], pr.at[y, e], m_send.at[i], m_recv.at[i], (asker(e), tp))

    def ml_copy(e):
        i = e - NEAR
        return remote(fl.at[i], lr.at[y, e], ml_send.at[i], ml_recv.at[i], (asker(e), tp))

    def prefix(d):
        yy = block_of(d)
        each(1, NEAR, lambda e: c_copy(d, e).wait_recv())
        for kk in range(ky):
            lanes = pl.ds(pl.multiple_of((yy * ky + kk) * HD, HD), HD)
            for j in range(SLOTS):
                part = slice(kk * strip + j * small, kk * strip + (j + 1) * small)
                asking = xr[yy, :, part, :].reshape(groups * small, HD)
                value, level = attend(nt(asking, pk[0, j, :, lanes]), pk[1, j, :, lanes])
                value = value.astype(jnp.bfloat16).reshape(groups, small, HD)
                po[yy, :, part, :] = value
                pr[yy, 0, part, :] = value[0]
                lc[:, part, :] = jnp.broadcast_to(level, (groups * small, 128)).reshape(
                    groups, small, 128
                )

        def pack(e):
            ls[yy, e] = jnp.broadcast_to(to_row(lc[e], lane_rows), (8, 128))

        each(0, groups, pack)
        lr[yy, 0] = ls[yy, 0]

        def send(e):
            e_copy(d, e).start()
            el_copy(d, e).start()

        each(1, NEAR, send)

    each(2, ys, ask)
    prefix(0)

    def prefix_step(i):
        d = turn(i)
        each(NEAR, groups, lambda e: f_copy(e, d).wait_recv())
        prefix(d)

        def send(e):
            r_copy(e, d).start()
            rl_copy(e, d).start()

        each(NEAR, groups, send)

    each(1, ys, prefix_step)

    def far_merge(e):
        i = e - NEAR

        def arrived(d):
            r_copy(e, d).wait_recv()
            rl_copy(e, d).wait_recv()

        each(1, ys, arrived)
        parts = [(po[y, e].astype(jnp.float32), to_column(ls[y, e, 0:1, :], lane_rows))]
        for d in range(1, ys):
            parts.append((fr[d, i].astype(jnp.float32), to_column(flr[d, i, 0:1, :], lane_rows)))
        value, level = merge(parts)
        fo[i] = value.astype(jnp.bfloat16)
        fl[i] = jnp.broadcast_to(to_row(level, lane_rows), (8, 128))
        m_copy(e).start()
        ml_copy(e).start()

    def y_copy(d):
        return remote(yb.at[block_of(d)], yr.at[d], y_send.at[d], y_recv.at[d], y_back(d))

    def yl_copy(d):
        return remote(yl.at[block_of(d)], ylr.at[d], yl_send.at[d], yl_recv.at[d], y_back(d))

    def join(d, owners):
        yy = block_of(d)

        def arrived(e):
            e_copy(d, e).wait_recv()
            el_copy(d, e).wait_recv()

        each(1, NEAR, arrived)
        levels = jnp.full((n, 128), MASKED, jnp.float32)
        for e in range(owners):
            levels = jnp.where(gsel[...] == owner(e), lr[yy, e, 0:1, :], levels)
        for kk in range(ky):
            hit = iota((n, 128), 1) == lsel[...] + kk * strip
            level = jnp.sum(jnp.where(hit, levels, 0.0), axis=1, keepdims=True)
            parts = pr[yy, 0:owners, kk * strip : (kk + 1) * strip, :].reshape(owners * strip, HD)
            k = yy * ky + kk
            value, joint = merge(
                [
                    (mm(back[:, 0 : owners * strip], parts), level),
                    (so[k].reshape(n, HD), sl[k].reshape(n, 128)[:, 0:1]),
                ]
            )
            yb[yy, kk * n : (kk + 1) * n, :] = value.astype(jnp.bfloat16)
            for i in range(n // 128):
                at = kk * (n // 128) + i
                yl[yy, at : at + 1, :] = to_row(joint[i * 128 : (i + 1) * 128], 128)

    def y_step(i):
        d = turn(i)
        join(d, NEAR)
        y_copy(d).start()
        yl_copy(d).start()

    each(1, ys - 1, y_step)
    each(NEAR, groups, far_merge)
    y_step(ys - 1)

    def far_arrived(e):
        m_copy(e).wait_recv()
        ml_copy(e).wait_recv()

    each(NEAR, groups, far_arrived)
    join(0, groups)

    def y_arrived(d):
        y_copy(d).wait_recv()
        yl_copy(d).wait_recv()

    each(1, ys, y_arrived)

    def y_merge(i):
        rows_at = pl.ds(pl.multiple_of(i * 128, 128), 128)
        parts = [(yb[y, rows_at, :].astype(jnp.float32), to_column(yl[y, pl.ds(i, 1), :], 128))]
        for d in range(1, ys):
            parts.append(
                (yr[d, rows_at, :].astype(jnp.float32), to_column(ylr[d, pl.ds(i, 1), :], 128))
            )
        value, level = merge(parts)
        zb[pl.ds(i * 2, 2)] = value.astype(jnp.bfloat16).reshape(2, 64, HD)
        zl[pl.ds(i * 2, 2)] = jnp.broadcast_to(to_row(level, 128)[None], (2, 8, 128))

    each(0, zs // 2, y_merge)

    def z_copy(d):
        return remote(zb.at[rem(z + d, zs)], zr.at[d], z_send.at[d], z_recv.at[d], z_peer(d))

    def zl_copy(d):
        return remote(zl.at[rem(z + d, zs)], zlr.at[d], zl_send.at[d], zl_recv.at[d], z_peer(d))

    def z_start(d):
        z_copy(d).start()
        zl_copy(d).start()

    each(0, zs - 1, lambda i: z_start(outward(i, zs)))

    def z_arrived(d):
        z_copy(d).wait_recv()
        zl_copy(d).wait_recv()

    each(1, zs, z_arrived)
    shift = rem(z, 2) * 64
    parts = [(zb[z].astype(jnp.float32), to_column(zl[z, 0:1, :], 64, shift))]
    for d in range(1, zs):
        parts.append((zr[d].astype(jnp.float32), to_column(zlr[d, 0:1, :], 64, shift)))
    attended = merge(parts)[0].astype(jnp.bfloat16)
    attended = jnp.concatenate([attended[0:rows], attended[rows : 2 * rows]], axis=1)

    loads[6].wait()
    span = zs // 2

    def z_order(i):
        return rem(outward(i, zs), zs)

    def wy_copy(h, d):
        part = pl.ds(h * span, span)
        return remote(
            wp.at[block_of(d), part], wr.at[d, part], wy_send.at[h, d], wy_recv.at[h, d], y_back(d)
        )

    def project(h, d):
        yy = block_of(d)

        def piece(i):
            columns = (yy * zs + rem(z + z_order(i), zs)) * (OWN * HD)
            columns = pl.ds(pl.multiple_of(columns, OWN * HD), OWN * HD)
            wp[yy, i] = mm(attended, wv[:, columns]).astype(jnp.bfloat16)

        for i in range(h * span, (h + 1) * span):
            piece(i)

    for h in (0, 1):
        def project_step(i, h=h):
            d = outward(i, ys)
            project(h, d)
            wy_copy(h, d).start()

        each(0, ys - 1, project_step)
        project(h, 0)

    def wz_copy(i):
        return remote(wz.at[i], wzr.at[i], wz_send.at[i], wz_recv.at[i], z_peer(z_order(i)))

    def y_sum(i):
        total = wp[y, i].astype(jnp.float32)
        for d in range(1, ys):
            total += wr[d, i].astype(jnp.float32)
        return total

    def w_step(i):
        wz[i] = y_sum(i).astype(jnp.bfloat16)
        wz_copy(i).start()

    each(1, ys, lambda d: wy_copy(0, d).wait_recv())
    each(0, span, w_step)
    each(1, ys, lambda d: wy_copy(1, d).wait_recv())
    each(span, zs - 1, w_step)
    total = y_sum(zs - 1)
    each(0, zs - 1, lambda i: wz_copy(i).wait_recv())
    for i in range(zs - 1):
        total += wzr[i].astype(jnp.float32)
    out_ref[...] = total.astype(jnp.bfloat16)

    def z_sent(d):
        a_copy(d).wait_send()
        z_copy(d).wait_send()
        zl_copy(d).wait_send()
        wz_copy(d - 1).wait_send()

    each(1, zs, z_sent)

    def y_sent(d):
        each(0, zs, lambda i: b_copy(i, d).wait_send())
        y_copy(d).wait_send()
        yl_copy(d).wait_send()
        wy_copy(0, d).wait_send()
        wy_copy(1, d).wait_send()

    each(1, ys, y_sent)

    def near_sent(d):
        def one(e):
            c_copy(d, e).wait_send()
            e_copy(d, e).wait_send()
            el_copy(d, e).wait_send()

        each(1, NEAR, one)

    def far_sent(e):
        def one(d):
            f_copy(e, d).wait_send()
            r_copy(e, d).wait_send()
            rl_copy(e, d).wait_send()

        c_copy(0, e).wait_send()
        each(1, ys, one)
        m_copy(e).wait_send()
        ml_copy(e).wait_send()

    each(0, ys, near_sent)
    each(NEAR, groups, far_sent)


def body(zs, queries, prefix_ids, suffix_lengths, owner_slots, prefix_cache, suffix_cache, wo):
    groups = lax.axis_size("grp")
    shards = lax.axis_size("tp")
    ys = shards // zs
    rows = queries.shape[0]
    suf = suffix_cache.shape[2]
    kvh = prefix_cache.shape[3] // HD
    size = shards * OWN // kvh
    n = size * rows
    ky = kvh // ys
    strip = SLOTS * size * CAP
    lane_rows = ky * strip
    far = groups - NEAR

    dims = (groups, ys, zs, kvh, rows, suf)
    bf, f32 = jnp.bfloat16, jnp.float32
    dma = pltpu.SemaphoreType.DMA
    vmem = pl.BlockSpec(memory_space=pltpu.VMEM)
    hbm = pl.BlockSpec(memory_space=pltpu.HBM)
    V = pltpu.VMEM
    scratch = [
        V(queries.shape, bf),
        V((1, rows), jnp.int32),
        V((1, rows), jnp.int32),
        V((1, owner_slots.shape[0]), jnp.int32),
        V(prefix_cache.shape, bf),
        V((2, rows * suf, kvh * HD), bf),
        V(wo.shape, bf),
        V((shards, OWN * rows, HD), bf),
        V((ys, groups, lane_rows, HD), bf),
        V((ys, groups, lane_rows, HD), bf),
        V((ys, groups, lane_rows, HD), bf),
        V((ys, groups, lane_rows, HD), bf),
        V((ys, groups, 8, 128), f32),
        V((ys, groups, 8, 128), f32),
        V((ys, far, lane_rows, HD), bf),
        V((ys, far, 8, 128), f32),
        V((far, lane_rows, HD), bf),
        V((far, 8, 128), f32),
        V((groups, lane_rows, 128), f32),
        V((kvh, size, rows, HD), f32),
        V((kvh, size, rows, 128), f32),
        V((groups * strip, n), bf),
        V((n, groups * strip), bf),
        V((n, 128), jnp.int32),
        V((n, 128), jnp.int32),
        V((2, n // 2, rows * suf // 2), f32),
        V((ys, ky * n, HD), bf),
        V((ys, 8, 128), f32),
        V((ys, ky * n, HD), bf),
        V((ys, 8, 128), f32),
        V((zs, OWN * rows, HD), bf),
        V((zs, 8, 128), f32),
        V((zs, OWN * rows, HD), bf),
        V((zs, 8, 128), f32),
        V((ys, zs, rows, OWN * HD), bf),
        V((ys, zs, rows, OWN * HD), bf),
        V((zs, rows, OWN * HD), bf),
        V((zs, rows, OWN * HD), bf),
        dma((7,)),
        dma((zs,)), dma((zs,)),
        dma((zs, ys)), dma((zs, ys)),
        dma((ys, groups)), dma((ys, groups)),
        dma((far, ys)), dma((far, ys)),
        dma((ys, groups)), dma((ys, groups)),
        dma((ys, groups)), dma((ys, groups)),
        dma((far, ys)), dma((far, ys)),
        dma((far, ys)), dma((far, ys)),
        dma((far,)), dma((far,)),
        dma((far,)), dma((far,)),
        dma((ys,)), dma((ys,)), dma((ys,)), dma((ys,)),
        dma((zs,)), dma((zs,)), dma((zs,)), dma((zs,)),
        dma((2, ys)), dma((2, ys)),
        dma((zs,)), dma((zs,)),
    ]
    return pl.pallas_call(
        functools.partial(kernel, dims),
        out_shape=jax.ShapeDtypeStruct((rows, wo.shape[1] // shards), bf),
        in_specs=[hbm] * 7,
        out_specs=vmem,
        scratch_shapes=scratch,
        compiler_params=pltpu.CompilerParams(
            collective_id=0, has_side_effects=True, vmem_limit_bytes=62 * 1024 * 1024
        ),
        name="decode_attention",
    )(
        queries, prefix_ids.reshape(1, rows), suffix_lengths.reshape(1, rows),
        owner_slots.reshape(1, -1), prefix_cache,
        suffix_cache.reshape(2, rows * suf, kvh * HD), wo,
    )


def solution(mesh, zs=Z_SIZE):
    placed = (
        P("grp", "tp"),
        P("grp", None),
        P("grp"),
        P(),
        P(None, "grp", "tp", None),
        P(None, "grp", "tp", None),
        P("tp", None),
    )
    return jax.shard_map(
        functools.partial(body, zs),
        mesh=mesh, in_specs=placed, out_specs=P("grp", "tp"), check_vma=False,
    )
```

```python
import functools
import math

import jax
import jax.numpy as jnp
from jax import lax
from jax.experimental import pallas as pl
from jax.experimental.pallas import tpu as pltpu
from jax.sharding import PartitionSpec as P

HD = 128
OWN = 2
SLOTS = 2
CAP = 4
LANES = SLOTS * CAP
Z_SIZE = 8
NEAR = 6
MASKED = -1e30
MESH = pl.DeviceIdType.MESH


def div(a, b):
    return a // b if isinstance(a, int) else lax.div(a, jnp.full_like(a, b))


def rem(a, b):
    return a % b if isinstance(a, int) else lax.rem(a, jnp.full_like(a, b))


def turn(i):
    return i + div(i, 2) * (1 - 2 * rem(i, 2))


def outward(i, count):
    return count // 2 + (1 - 2 * rem(i, 2)) * div(i + 1, 2)


def nt(a, b):
    return lax.dot_general(a, b, (((1,), (1,)), ((), ())), preferred_element_type=jnp.float32)


def mm(a, b):
    return jnp.dot(a, b, preferred_element_type=jnp.float32)


def iota(shape, dim):
    return lax.broadcasted_iota(jnp.int32, shape, dim)


def diagonal(rows, shift=0):
    return iota((rows, 128), 1) == iota((rows, 128), 0) + shift


def to_row(column, rows):
    wide = jnp.broadcast_to(column, (rows, 128))
    return jnp.sum(jnp.where(diagonal(rows), wide, 0.0), axis=0, keepdims=True)


def to_column(row, rows, shift=0):
    wide = jnp.broadcast_to(row, (rows, 128))
    return jnp.sum(jnp.where(diagonal(rows, shift), wide, 0.0), axis=1, keepdims=True)


def merge(parts):
    largest = functools.reduce(jnp.maximum, [level for _, level in parts])
    factors = [jnp.exp(level - largest) for _, level in parts]
    total = functools.reduce(jnp.add, factors)
    summed = functools.reduce(jnp.add, [f * value for f, (value, _) in zip(factors, parts)])
    return summed / total, largest + jnp.log(total)


def spread(row, shape, index):
    return jnp.sum(jnp.where(iota(shape, 1) == index, row, 0.0), axis=1, keepdims=True)


def attend(products, values):
    scale = 1.0 / math.sqrt(HD)
    highest = jnp.max(products, axis=1, keepdims=True)
    weights = jnp.exp((products - highest) * scale)
    totals = jnp.sum(weights, axis=1, keepdims=True)
    summed = mm(weights.astype(jnp.bfloat16), values)
    return summed / totals, highest * scale + jnp.log(totals)


def kernel(
    dims,
    q_ref, ids_ref, len_ref, slots_ref, pc_ref, sc_ref, wo_ref, out_ref,
    qv, idv, lenv, slotv, pk, sk, wv, qall, xs, xr, po, pr, ls, lr, fr, flr, fo, fl, lc, so, sl, sel, back, gsel, lsel, bias,
    yb, yl, yr, ylr, ur, ulr, vb, vl, vr, vlr, zb, zl, zr, zlr, wp, wr, wz, wzr, wur, wvb, wvr,
    in_sem, a_send, a_recv, b_send, b_recv, o_send, o_recv, w_send, w_recv, c_send, c_recv, f_send, f_recv,
    e_send, e_recv, el_send, el_recv, r_send, r_recv, rl_send, rl_recv, m_send, m_recv, ml_send, ml_recv,
    y_send, y_recv, yl_send, yl_recv, z_send, z_recv, zl_send, zl_recv,
    u_send, u_recv, ul_send, ul_recv, v_send, v_recv, wu_send, wu_recv, wv_send, wv_recv,
    wy_send, wy_recv, wz_send, wz_recv,
):
    groups, ys, zs, kvh, rows, suf = dims
    ky = kvh // ys
    dk = ys * zs // kvh
    size = dk * OWN
    n = size * rows
    strip = SLOTS * size * CAP
    lane_rows = ky * strip
    small = size * CAP
    half = rows // 2
    grp = lax.axis_index("grp")
    tp = lax.axis_index("tp")
    y = div(tp, zs)
    z = rem(tp, zs)

    opposite = ys // 2
    beside = [d for d in range(1, ys) if d != opposite]

    def remote(src, dst, send, recv, device):
        return pltpu.make_async_remote_copy(
            src_ref=src, dst_ref=dst, send_sem=send, recv_sem=recv,
            device_id=device, device_id_type=MESH,
        )

    def each(low, high, fn):
        def step(i, c):
            fn(i)
            return c
        lax.fori_loop(low, high, step, 0)

    loads = [
        pltpu.make_async_copy(q_ref, qv, in_sem.at[0]),
        pltpu.make_async_copy(ids_ref, idv, in_sem.at[1]),
        pltpu.make_async_copy(len_ref, lenv, in_sem.at[2]),
        pltpu.make_async_copy(slots_ref, slotv, in_sem.at[3]),
        pltpu.make_async_copy(sc_ref, sk, in_sem.at[4]),
        pltpu.make_async_copy(pc_ref, pk, in_sem.at[5]),
        pltpu.make_async_copy(wo_ref, wv, in_sem.at[6]),
    ]
    for load in loads:
        load.start()

    def z_peer(d):
        return (grp, y * zs + rem(z + d, zs))

    def y_peer(d):
        return (grp, rem(y + d, ys) * zs + z)

    def y_back(d):
        return (grp, rem(y - d + ys, ys) * zs + z)

    def owner(e):
        x, core = rem(div(grp, 2) + turn(div(e, 2)), groups // 2), rem(grp + e, 2)
        return x * 2 + core

    def asker(e):
        x, core = rem(div(grp, 2) + groups // 2 - turn(div(e, 2)), groups // 2), rem(grp + e, 2)
        return x * 2 + core

    barrier = pltpu.get_barrier_semaphore()
    each(1, zs, lambda d: pl.semaphore_signal(barrier, inc=1, device_id=z_peer(d), device_id_type=MESH))
    each(1, ys, lambda d: pl.semaphore_signal(barrier, inc=1, device_id=y_peer(d), device_id_type=MESH))
    each(1, groups, lambda d: pl.semaphore_signal(barrier, inc=1, device_id=(owner(d), tp), device_id_type=MESH))

    loads[0].wait()
    qall[tp, 0:rows, :] = qv[:, 0:HD]
    qall[tp, rows : 2 * rows, :] = qv[:, HD : 2 * HD]
    pl.semaphore_wait(barrier, zs + ys + groups - 3)

    def a_copy(d):
        return remote(qall.at[tp], qall.at[tp], a_send.at[d], a_recv.at[d], z_peer(d))

    def b_copy(d):
        row = qall.at[pl.ds(y * zs, zs)]
        return remote(row, row, b_send.at[d], b_recv.at[d], y_peer(d))

    def o_copy():
        return remote(qall.at[tp], qall.at[tp], o_send.at[0], o_recv.at[0], y_peer(opposite))

    def w_copy(d):
        piece = qall.at[rem(y + opposite, ys) * zs + z]
        return remote(piece, piece, w_send.at[d], w_recv.at[d], z_peer(d))

    each(0, zs - 1, lambda i: a_copy(outward(i, zs)).start())
    o_copy().start()

    for load in loads[1:4]:
        load.wait()
    ids = idv[...].astype(jnp.float32)
    lengths = lenv[...].astype(jnp.float32)
    slot_count = slotv.shape[1]
    slots = spread(slotv[...].astype(jnp.float32), (slot_count,) * 2, iota((slot_count,) * 2, 0))
    square = (rows, rows)
    ids_column = spread(ids, square, iota(square, 0))
    slot_of = jnp.sum(
        jnp.where(iota((slot_count, rows), 0).astype(jnp.float32) == ids, slots, 0.0),
        axis=0, keepdims=True,
    )
    earlier = (ids_column == ids) & (iota(square, 0) < iota(square, 1))
    target = slot_of * CAP + jnp.sum(jnp.where(earlier, 1.0, 0.0), axis=0, keepdims=True)
    target_column = spread(target, square, iota(square, 0))
    all_rows = jnp.sum(
        jnp.where(iota((rows, n), 0) == rem(iota((rows, n), 1), rows), target_column, 0.0),
        axis=0, keepdims=True,
    ).astype(jnp.int32) + (groups * LANES) * (div(iota((1, n), 1), rows))
    all_column = spread(target, (n, rows), rem(iota((n, rows), 0), rows)).astype(jnp.int32)
    head = div(iota((n, 128), 0), rows)
    place = jnp.broadcast_to(all_column, (n, 128))
    gsel[...] = div(place, LANES)
    lsel[...] = rem(div(place, CAP), SLOTS) * small + head * CAP + rem(place, CAP)
    wide = groups * strip

    def lane_code(i):
        lane = rem(div(i, small), SLOTS) * CAP + rem(i, CAP)
        return owner(div(i, strip)) * LANES + lane + groups * LANES * rem(div(i, CAP), size)

    sel[...] = jnp.where(lane_code(iota((wide, n), 0)) == all_rows, 1.0, 0.0).astype(jnp.bfloat16)
    back[...] = jnp.where(
        lane_code(iota((n, wide), 1)) == all_column + (groups * LANES) * div(iota((n, 1), 0), rows),
        1.0, 0.0,
    ).astype(jnp.bfloat16)
    box = (size * half, half * suf)
    for h in range(2):
        limit = spread(lengths, (size * half, rows), rem(iota((size * half, rows), 0), half) + h * half)
        kept = (div(iota(box, 1), suf) == rem(iota(box, 0), half)) & (
            rem(iota(box, 1), suf) + tp * suf < limit.astype(jnp.int32)
        )
        bias[h] = jnp.where(kept, 0.0, MASKED)

    o_copy().wait_recv()
    each(0, zs - 1, lambda i: w_copy(outward(i, zs)).start())
    each(1, zs, lambda d: a_copy(d).wait_recv())
    for d in beside:
        b_copy(d).start()

    def block_of(d):
        return rem(y - d + ys, ys)

    def c_copy(d, e):
        yy = block_of(d)
        return remote(
            xs.at[yy, e], xr.at[yy, e], c_send.at[d, e], c_recv.at[d, e], (owner(e), tp)
        )

    def c_stage(d):
        yy = block_of(d)
        for kk in range(ky):
            part = slice(kk * strip, (kk + 1) * strip)
            block = qall[pl.ds((yy * ky + kk) * dk, dk)].reshape(n, HD)
            picked = mm(sel[...], block).astype(jnp.bfloat16).reshape(groups, strip, HD)
            xs[yy, :, part, :] = picked
            xr[yy, 0, part, :] = picked[0]

    def f_copy(e, d):
        return remote(
            xr.at[y, e], xr.at[y, e], f_send.at[e - NEAR, d], f_recv.at[e - NEAR, d], y_peer(d)
        )

    def suffix(k):
        lanes = pl.ds(pl.multiple_of(k * HD, HD), HD)
        block = qall[pl.ds(k * dk, dk)].reshape(size, rows, HD)
        for h in range(2):
            part = slice(h * half, (h + 1) * half)
            at = slice(h * half * suf, (h + 1) * half * suf)
            asking = block[:, part, :].reshape(size * half, HD)
            value, level = attend(nt(asking, sk[0, at, lanes]) + bias[h], sk[1, at, lanes])
            so[k, :, part, :] = value.reshape(size, half, HD)
            sl[k, :, part, :] = jnp.broadcast_to(level, (size * half, 128)).reshape(size, half, 128)

    def suffixes(d):
        yy = block_of(d)
        for kk in range(ky):
            suffix(yy * ky + kk)

    c_stage(0)
    each(1, groups, lambda e: c_copy(0, groups - e).start())
    loads[4].wait()
    suffixes(0)

    def ask(d):
        if d == opposite:
            each(1, zs, lambda i: w_copy(i).wait_recv())
        else:
            b_copy(d).wait_recv()
        c_stage(d)
        each(1, NEAR, lambda e: c_copy(d, e).start())
        suffixes(d)

    def pass_on(e):
        c_copy(0, e).wait_recv()
        each(1, ys, lambda d: f_copy(e, d).start())

    order = [opposite] + beside
    ask(order[0])
    each(NEAR, groups, pass_on)

    loads[5].wait()

    def e_copy(d, e):
        yy = block_of(d)
        return remote(
            po.at[yy, e], pr.at[yy, e], e_send.at[d, e], e_recv.at[d, e], (asker(e), tp)
        )

    def el_copy(d, e):
        yy = block_of(d)
        return remote(
            ls.at[yy, e], lr.at[yy, e], el_send.at[d, e], el_recv.at[d, e], (asker(e), tp)
        )

    def r_copy(e, d):
        i = e - NEAR
        return remote(
            po.at[block_of(d), e], fr.at[d, i], r_send.at[i, d], r_recv.at[i, d], y_back(d)
        )

    def rl_copy(e, d):
        i = e - NEAR
        return remote(
            ls.at[block_of(d), e], flr.at[d, i], rl_send.at[i, d], rl_recv.at[i, d], y_back(d)
        )

    def m_copy(e):
        i = e - NEAR
        return remote(fo.at[i], pr.at[y, e], m_send.at[i], m_recv.at[i], (asker(e), tp))

    def ml_copy(e):
        i = e - NEAR
        return remote(fl.at[i], lr.at[y, e], ml_send.at[i], ml_recv.at[i], (asker(e), tp))

    def prefix(d):
        yy = block_of(d)
        each(1, NEAR, lambda e: c_copy(d, e).wait_recv())
        for kk in range(ky):
            lanes = pl.ds(pl.multiple_of((yy * ky + kk) * HD, HD), HD)
            for j in range(SLOTS):
                part = slice(kk * strip + j * small, kk * strip + (j + 1) * small)
                asking = xr[yy, :, part, :].reshape(groups * small, HD)
                value, level = attend(nt(asking, pk[0, j, :, lanes]), pk[1, j, :, lanes])
                value = value.astype(jnp.bfloat16).reshape(groups, small, HD)
                po[yy, :, part, :] = value
                pr[yy, 0, part, :] = value[0]
                lc[:, part, :] = jnp.broadcast_to(level, (groups * small, 128)).reshape(
                    groups, small, 128
                )

        for e in range(groups):
            ls[yy, e] = jnp.broadcast_to(to_row(lc[e], lane_rows), (8, 128))
        lr[yy, 0] = ls[yy, 0]

        def send(e):
            e_copy(d, e).start()
            el_copy(d, e).start()

        each(1, NEAR, send)

    for d in order[1:]:
        ask(d)
    prefix(0)

    def prefix_step(i):
        d = outward(i - 1, ys)
        each(NEAR, groups, lambda e: f_copy(e, d).wait_recv())
        prefix(d)

        def send(e):
            r_copy(e, d).start()
            rl_copy(e, d).start()

        each(NEAR, groups, send)

    each(1, ys, prefix_step)

    def far_merge(e):
        i = e - NEAR

        def arrived(d):
            r_copy(e, d).wait_recv()
            rl_copy(e, d).wait_recv()

        each(1, ys, arrived)
        parts = [(po[y, e].astype(jnp.float32), to_column(ls[y, e, 0:1, :], lane_rows))]
        for d in range(1, ys):
            parts.append((fr[d, i].astype(jnp.float32), to_column(flr[d, i, 0:1, :], lane_rows)))
        value, level = merge(parts)
        fo[i] = value.astype(jnp.bfloat16)
        fl[i] = jnp.broadcast_to(to_row(level, lane_rows), (8, 128))
        m_copy(e).start()
        ml_copy(e).start()

    def y_copy(d):
        return remote(yb.at[block_of(d)], yr.at[d], y_send.at[d], y_recv.at[d], y_back(d))

    def yl_copy(d):
        return remote(yl.at[block_of(d)], ylr.at[d], yl_send.at[d], yl_recv.at[d], y_back(d))

    def join(d, owners):
        yy = block_of(d)

        def arrived(e):
            e_copy(d, e).wait_recv()
            el_copy(d, e).wait_recv()

        each(1, NEAR, arrived)
        levels = jnp.full((n, 128), MASKED, jnp.float32)
        for e in range(owners):
            levels = jnp.where(gsel[...] == owner(e), lr[yy, e, 0:1, :], levels)
        for kk in range(ky):
            hit = iota((n, 128), 1) == lsel[...] + kk * strip
            level = jnp.sum(jnp.where(hit, levels, 0.0), axis=1, keepdims=True)
            parts = pr[yy, 0:owners, kk * strip : (kk + 1) * strip, :].reshape(owners * strip, HD)
            k = yy * ky + kk
            value, joint = merge(
                [
                    (mm(back[:, 0 : owners * strip], parts), level),
                    (so[k].reshape(n, HD), sl[k].reshape(n, 128)[:, 0:1]),
                ]
            )
            yb[yy, kk * dk : (kk + 1) * dk] = value.astype(jnp.bfloat16).reshape(dk, OWN * rows, HD)
            for i in range(dk // 2):
                row = to_row(joint[i * 128 : (i + 1) * 128], 128)
                yl[yy, kk * dk // 2 + i] = jnp.broadcast_to(row, (8, 128))

    across = rem(y + opposite, ys)

    def u_copy(d):
        return remote(yb.at[across, rem(z + d, zs)], ur.at[d], u_send.at[d], u_recv.at[d], z_peer(d))

    def ul_copy(d):
        return remote(
            yl.at[across, div(rem(z + d, zs), 2)], ulr.at[d], ul_send.at[d], ul_recv.at[d], z_peer(d)
        )

    def v_copy():
        return remote(vb, vr, v_send.at[0], v_recv.at[0], y_peer(opposite))

    def vl_copy():
        return remote(vl, vlr, v_send.at[1], v_recv.at[1], y_peer(opposite))

    def u_start(i):
        d = outward(i, zs)
        u_copy(d).start()
        ul_copy(d).start()

    join(opposite, NEAR)
    each(0, zs - 1, u_start)
    for d in beside:
        join(d, NEAR)
        y_copy(d).start()
        yl_copy(d).start()
    each(NEAR, groups, far_merge)

    def far_arrived(e):
        m_copy(e).wait_recv()
        ml_copy(e).wait_recv()

    each(NEAR, groups, far_arrived)
    join(0, groups)

    def u_arrived(d):
        u_copy(d).wait_recv()
        ul_copy(d).wait_recv()

    each(1, zs, u_arrived)
    shift = rem(z, 2) * 64
    parts = [(yb[across, z].astype(jnp.float32), to_column(yl[across, div(z, 2), 0:1, :], 64, shift))]
    for d in range(1, zs):
        parts.append((ur[d].astype(jnp.float32), to_column(ulr[d, 0:1, :], 64, shift)))
    value, level = merge(parts)
    vb[...] = value.astype(jnp.bfloat16)
    vl[...] = jnp.broadcast_to(to_row(level, 64), (8, 128))
    v_copy().start()
    vl_copy().start()

    def y_arrived(d):
        y_copy(d).wait_recv()
        yl_copy(d).wait_recv()

    for d in beside:
        y_arrived(d)

    def y_merge(i):
        pair = pl.ds(i * 2, 2)
        parts = [(yb[y, pair].reshape(128, HD).astype(jnp.float32), to_column(yl[y, i, 0:1, :], 128))]
        for d in beside:
            value = yr[d, pair].reshape(128, HD).astype(jnp.float32)
            parts.append((value, to_column(ylr[d, i, 0:1, :], 128)))
        value, level = merge(parts)
        zb[pair] = value.astype(jnp.bfloat16).reshape(2, 64, HD)
        zl[pair] = jnp.broadcast_to(to_row(level, 128)[None], (2, 8, 128))

    each(0, zs // 2, y_merge)

    def z_copy(d):
        return remote(zb.at[rem(z + d, zs)], zr.at[d], z_send.at[d], z_recv.at[d], z_peer(d))

    def zl_copy(d):
        return remote(zl.at[rem(z + d, zs)], zlr.at[d], zl_send.at[d], zl_recv.at[d], z_peer(d))

    def z_start(d):
        z_copy(d).start()
        zl_copy(d).start()

    each(0, zs - 1, lambda i: z_start(outward(i, zs)))

    def z_arrived(d):
        z_copy(d).wait_recv()
        zl_copy(d).wait_recv()

    each(1, zs, z_arrived)
    v_copy().wait_recv()
    vl_copy().wait_recv()
    parts = [
        (zb[z].astype(jnp.float32), to_column(zl[z, 0:1, :], 64, shift)),
        (vr[...].astype(jnp.float32), to_column(vlr[0:1, :], 64)),
    ]
    for d in range(1, zs):
        parts.append((zr[d].astype(jnp.float32), to_column(zlr[d, 0:1, :], 64, shift)))
    attended = merge(parts)[0].astype(jnp.bfloat16)
    attended = jnp.concatenate([attended[0:rows], attended[rows : 2 * rows]], axis=1)

    loads[6].wait()

    def z_order(i):
        return rem(outward(i, zs), zs)

    span = zs // 2

    def wy_copy(h, d):
        part = pl.ds(h * span, span)
        return remote(
            wp.at[block_of(d), part], wr.at[d, part], wy_send.at[h, d], wy_recv.at[h, d], y_back(d)
        )

    def wu_copy(i):
        return remote(
            wp.at[across, i], wur.at[i], wu_send.at[i], wu_recv.at[i], z_peer(z_order(i))
        )

    def wv_copy():
        return remote(wvb, wvr, wv_send.at[0], wv_recv.at[0], y_peer(opposite))

    def wz_copy(i):
        return remote(wz.at[i], wzr.at[i], wz_send.at[i], wz_recv.at[i], z_peer(z_order(i)))

    def project(h, d):
        yy = block_of(d)
        for i in range(h * span, (h + 1) * span):
            columns = (yy * zs + rem(z + z_order(i), zs)) * (OWN * HD)
            columns = pl.ds(pl.multiple_of(columns, OWN * HD), OWN * HD)
            wp[yy, i] = mm(attended, wv[:, columns]).astype(jnp.bfloat16)

    for h in range(2):
        project(h, opposite)
        each(h * span, min((h + 1) * span, zs - 1), lambda i: wu_copy(i).start())
        for d in beside:
            project(h, d)
            wy_copy(h, d).start()
    project(0, 0)
    project(1, 0)
    def y_sum(i):
        total = wp[y, i].astype(jnp.float32)
        for d in beside:
            total += wr[d, i].astype(jnp.float32)
        return total

    def w_step(i):
        wz[i] = y_sum(i).astype(jnp.bfloat16)
        wz_copy(i).start()

    def z_sent(d):
        a_copy(d).wait_send()
        z_copy(d).wait_send()
        zl_copy(d).wait_send()
        w_copy(d).wait_send()
        u_copy(d).wait_send()
        ul_copy(d).wait_send()

    each(1, zs, z_sent)

    for d in beside:
        b_copy(d).wait_send()
        y_copy(d).wait_send()
        yl_copy(d).wait_send()
    o_copy().wait_send()
    v_copy().wait_send()
    vl_copy().wait_send()

    def near_sent(d):
        def one(e):
            c_copy(d, e).wait_send()
            e_copy(d, e).wait_send()
            el_copy(d, e).wait_send()

        each(1, NEAR, one)

    def far_sent(e):
        def one(d):
            f_copy(e, d).wait_send()
            r_copy(e, d).wait_send()
            rl_copy(e, d).wait_send()

        c_copy(0, e).wait_send()
        each(1, ys, one)
        m_copy(e).wait_send()
        ml_copy(e).wait_send()

    each(0, ys, near_sent)
    each(NEAR, groups, far_sent)

    for d in beside:
        wy_copy(0, d).wait_recv()
    each(0, span, w_step)
    each(0, zs - 1, lambda i: wu_copy(i).wait_recv())
    total = wp[across, zs - 1].astype(jnp.float32)
    for i in range(zs - 1):
        total += wur[i].astype(jnp.float32)
    wvb[...] = total.astype(jnp.bfloat16)
    wv_copy().start()
    for d in beside:
        wy_copy(1, d).wait_recv()
    each(span, zs - 1, w_step)
    total = y_sum(zs - 1)
    wv_copy().wait_recv()
    total += wvr[...].astype(jnp.float32)
    each(0, zs - 1, lambda i: wz_copy(i).wait_recv())
    for i in range(zs - 1):
        total += wzr[i].astype(jnp.float32)
    out_ref[...] = total.astype(jnp.bfloat16)

    def last_sent(i):
        wu_copy(i).wait_send()
        wz_copy(i).wait_send()

    each(0, zs - 1, last_sent)
    for d in beside:
        wy_copy(0, d).wait_send()
        wy_copy(1, d).wait_send()
    wv_copy().wait_send()


def body(zs, queries, prefix_ids, suffix_lengths, owner_slots, prefix_cache, suffix_cache, wo):
    groups = lax.axis_size("grp")
    shards = lax.axis_size("tp")
    ys = shards // zs
    rows = queries.shape[0]
    suf = suffix_cache.shape[2]
    kvh = prefix_cache.shape[3] // HD
    size = shards * OWN // kvh
    n = size * rows
    ky = kvh // ys
    strip = SLOTS * size * CAP
    lane_rows = ky * strip
    far = groups - NEAR

    dims = (groups, ys, zs, kvh, rows, suf)
    bf, f32 = jnp.bfloat16, jnp.float32
    dma = pltpu.SemaphoreType.DMA
    vmem = pl.BlockSpec(memory_space=pltpu.VMEM)
    hbm = pl.BlockSpec(memory_space=pltpu.HBM)
    V = pltpu.VMEM
    scratch = [
        V(queries.shape, bf),
        V((1, rows), jnp.int32),
        V((1, rows), jnp.int32),
        V((1, owner_slots.shape[0]), jnp.int32),
        V(prefix_cache.shape, bf),
        V((2, rows * suf, kvh * HD), bf),
        V(wo.shape, bf),
        V((shards, OWN * rows, HD), bf),
        V((ys, groups, lane_rows, HD), bf),
        V((ys, groups, lane_rows, HD), bf),
        V((ys, groups, lane_rows, HD), bf),
        V((ys, groups, lane_rows, HD), bf),
        V((ys, groups, 8, 128), f32),
        V((ys, groups, 8, 128), f32),
        V((ys, far, lane_rows, HD), bf),
        V((ys, far, 8, 128), f32),
        V((far, lane_rows, HD), bf),
        V((far, 8, 128), f32),
        V((groups, lane_rows, 128), f32),
        V((kvh, size, rows, HD), f32),
        V((kvh, size, rows, 128), f32),
        V((groups * strip, n), bf),
        V((n, groups * strip), bf),
        V((n, 128), jnp.int32),
        V((n, 128), jnp.int32),
        V((2, n // 2, rows * suf // 2), f32),
        V((ys, zs, OWN * rows, HD), bf),
        V((ys, zs // 2, 8, 128), f32),
        V((ys, zs, OWN * rows, HD), bf),
        V((ys, zs // 2, 8, 128), f32),
        V((zs, OWN * rows, HD), bf),
        V((zs, 8, 128), f32),
        V((OWN * rows, HD), bf),
        V((8, 128), f32),
        V((OWN * rows, HD), bf),
        V((8, 128), f32),
        V((zs, OWN * rows, HD), bf),
        V((zs, 8, 128), f32),
        V((zs, OWN * rows, HD), bf),
        V((zs, 8, 128), f32),
        V((ys, zs, rows, OWN * HD), bf),
        V((ys, zs, rows, OWN * HD), bf),
        V((zs, rows, OWN * HD), bf),
        V((zs, rows, OWN * HD), bf),
        V((zs, rows, OWN * HD), bf),
        V((rows, OWN * HD), bf),
        V((rows, OWN * HD), bf),
        dma((7,)),
        dma((zs,)), dma((zs,)),
        dma((ys,)), dma((ys,)),
        dma((1,)), dma((1,)),
        dma((zs,)), dma((zs,)),
        dma((ys, groups)), dma((ys, groups)),
        dma((far, ys)), dma((far, ys)),
        dma((ys, groups)), dma((ys, groups)),
        dma((ys, groups)), dma((ys, groups)),
        dma((far, ys)), dma((far, ys)),
        dma((far, ys)), dma((far, ys)),
        dma((far,)), dma((far,)),
        dma((far,)), dma((far,)),
        dma((ys,)), dma((ys,)), dma((ys,)), dma((ys,)),
        dma((zs,)), dma((zs,)), dma((zs,)), dma((zs,)),
        dma((zs,)), dma((zs,)), dma((zs,)), dma((zs,)),
        dma((2,)), dma((2,)),
        dma((zs,)), dma((zs,)),
        dma((1,)), dma((1,)),
        dma((2, ys)), dma((2, ys)),
        dma((zs,)), dma((zs,)),
    ]
    return pl.pallas_call(
        functools.partial(kernel, dims),
        out_shape=jax.ShapeDtypeStruct((rows, wo.shape[1] // shards), bf),
        in_specs=[hbm] * 7,
        out_specs=vmem,
        scratch_shapes=scratch,
        compiler_params=pltpu.CompilerParams(
            collective_id=0, has_side_effects=True, vmem_limit_bytes=62 * 1024 * 1024
        ),
        name="decode_attention",
    )(
        queries, prefix_ids.reshape(1, rows), suffix_lengths.reshape(1, rows),
        owner_slots.reshape(1, -1), prefix_cache,
        suffix_cache.reshape(2, rows * suf, kvh * HD), wo,
    )


def solution(mesh, zs=Z_SIZE):
    placed = (
        P("grp", "tp"),
        P("grp", None),
        P("grp"),
        P(),
        P(None, "grp", "tp", None),
        P(None, "grp", "tp", None),
        P("tp", None),
    )
    return jax.shard_map(
        functools.partial(body, zs),
        mesh=mesh, in_specs=placed, out_specs=P("grp", "tp"), check_vma=False,
    )
```

```python
import functools
import math

import jax
import jax.numpy as jnp
from jax import lax
from jax.experimental import pallas as pl
from jax.experimental.pallas import tpu as pltpu
from jax.sharding import PartitionSpec as P

HD = 128
OWN = 2
SLOTS = 2
CAP = 4
LANES = SLOTS * CAP
Z_SIZE = 8
NEAR = 6
MASKED = -1e30
MESH = pl.DeviceIdType.MESH


def div(a, b):
    return a // b if isinstance(a, int) else lax.div(a, jnp.full_like(a, b))


def rem(a, b):
    return a % b if isinstance(a, int) else lax.rem(a, jnp.full_like(a, b))


def turn(i):
    return i + div(i, 2) * (1 - 2 * rem(i, 2))


def outward(i, count):
    return count // 2 + (1 - 2 * rem(i, 2)) * div(i + 1, 2)


def nt(a, b):
    return lax.dot_general(a, b, (((1,), (1,)), ((), ())), preferred_element_type=jnp.float32)


def mm(a, b):
    return jnp.dot(a, b, preferred_element_type=jnp.float32)


def iota(shape, dim):
    return lax.broadcasted_iota(jnp.int32, shape, dim)


def diagonal(rows, shift=0):
    return iota((rows, 128), 1) == iota((rows, 128), 0) + shift


def to_row(column, rows):
    wide = jnp.broadcast_to(column, (rows, 128))
    return jnp.sum(jnp.where(diagonal(rows), wide, 0.0), axis=0, keepdims=True)


def to_column(row, rows, shift=0):
    wide = jnp.broadcast_to(row, (rows, 128))
    return jnp.sum(jnp.where(diagonal(rows, shift), wide, 0.0), axis=1, keepdims=True)


def merge(parts):
    largest = functools.reduce(jnp.maximum, [level for _, level in parts])
    factors = [jnp.exp(level - largest) for _, level in parts]
    total = functools.reduce(jnp.add, factors)
    summed = functools.reduce(jnp.add, [f * value for f, (value, _) in zip(factors, parts)])
    return summed / total, largest + jnp.log(total)


def spread(row, shape, index):
    return jnp.sum(jnp.where(iota(shape, 1) == index, row, 0.0), axis=1, keepdims=True)


def attend(products, values):
    scale = 1.0 / math.sqrt(HD)
    highest = jnp.max(products, axis=1, keepdims=True)
    weights = jnp.exp((products - highest) * scale)
    totals = jnp.sum(weights, axis=1, keepdims=True)
    summed = mm(weights.astype(jnp.bfloat16), values)
    return summed / totals, highest * scale + jnp.log(totals)


def kernel(
    dims,
    q_ref, ids_ref, len_ref, slots_ref, pc_ref, sc_ref, wo_ref, out_ref,
    qv, idv, lenv, slotv, pk, sk, wv, qall, xs, xr, po, pr, ls, lr, fr, flr, fo, fl, lc, so, sl, sel, back, gsel, lsel, bias,
    yb, yl, yr, ylr, ur, ulr, vb, vl, vr, vlr, zb, zl, zr, zlr, wp, wr, wz, wzr, wur, wvb, wvr,
    in_sem, a_send, a_recv, b_send, b_recv, o_send, o_recv, w_send, w_recv, c_send, c_recv, f_send, f_recv,
    e_send, e_recv, el_send, el_recv, r_send, r_recv, rl_send, rl_recv, m_send, m_recv, ml_send, ml_recv,
    y_send, y_recv, yl_send, yl_recv, z_send, z_recv, zl_send, zl_recv,
    u_send, u_recv, ul_send, ul_recv, v_send, v_recv, wu_send, wu_recv, wv_send, wv_recv,
    wy_send, wy_recv, wz_send, wz_recv,
):
    groups, ys, zs, kvh, rows, suf = dims
    ky = kvh // ys
    dk = ys * zs // kvh
    size = dk * OWN
    n = size * rows
    strip = SLOTS * size * CAP
    lane_rows = ky * strip
    small = size * CAP
    half = rows // 2
    grp = lax.axis_index("grp")
    tp = lax.axis_index("tp")
    y = div(tp, zs)
    z = rem(tp, zs)

    opposite = ys // 2
    beside = [d for d in range(1, ys) if d != opposite]

    def remote(src, dst, send, recv, device):
        return pltpu.make_async_remote_copy(
            src_ref=src, dst_ref=dst, send_sem=send, recv_sem=recv,
            device_id=device, device_id_type=MESH,
        )

    def each(low, high, fn):
        def step(i, c):
            fn(i)
            return c
        lax.fori_loop(low, high, step, 0)

    loads = [
        pltpu.make_async_copy(q_ref, qv, in_sem.at[0]),
        pltpu.make_async_copy(ids_ref, idv, in_sem.at[1]),
        pltpu.make_async_copy(len_ref, lenv, in_sem.at[2]),
        pltpu.make_async_copy(slots_ref, slotv, in_sem.at[3]),
        pltpu.make_async_copy(sc_ref, sk, in_sem.at[4]),
        pltpu.make_async_copy(pc_ref, pk, in_sem.at[5]),
        pltpu.make_async_copy(wo_ref, wv, in_sem.at[6]),
    ]
    for load in loads:
        load.start()

    def z_peer(d):
        return (grp, y * zs + rem(z + d, zs))

    def y_peer(d):
        return (grp, rem(y + d, ys) * zs + z)

    def y_back(d):
        return (grp, rem(y - d + ys, ys) * zs + z)

    def owner(e):
        x, core = rem(div(grp, 2) + turn(div(e, 2)), groups // 2), rem(grp + e, 2)
        return x * 2 + core

    def asker(e):
        x, core = rem(div(grp, 2) + groups // 2 - turn(div(e, 2)), groups // 2), rem(grp + e, 2)
        return x * 2 + core

    barrier = pltpu.get_barrier_semaphore()
    each(1, zs, lambda d: pl.semaphore_signal(barrier, inc=1, device_id=z_peer(d), device_id_type=MESH))
    each(1, ys, lambda d: pl.semaphore_signal(barrier, inc=1, device_id=y_peer(d), device_id_type=MESH))
    each(1, groups, lambda d: pl.semaphore_signal(barrier, inc=1, device_id=(owner(d), tp), device_id_type=MESH))

    loads[0].wait()
    qall[tp, 0:rows, :] = qv[:, 0:HD]
    qall[tp, rows : 2 * rows, :] = qv[:, HD : 2 * HD]
    pl.semaphore_wait(barrier, zs + ys + groups - 3)

    def a_copy(d):
        return remote(qall.at[tp], qall.at[tp], a_send.at[d], a_recv.at[d], z_peer(d))

    def b_copy(d):
        row = qall.at[pl.ds(y * zs, zs)]
        return remote(row, row, b_send.at[d], b_recv.at[d], y_peer(d))

    def o_copy():
        return remote(qall.at[tp], qall.at[tp], o_send.at[0], o_recv.at[0], y_peer(opposite))

    def w_copy(d):
        piece = qall.at[rem(y + opposite, ys) * zs + z]
        return remote(piece, piece, w_send.at[d], w_recv.at[d], z_peer(d))

    each(0, zs - 1, lambda i: a_copy(outward(i, zs)).start())
    o_copy().start()

    for load in loads[1:4]:
        load.wait()
    ids = idv[...].astype(jnp.float32)
    lengths = lenv[...].astype(jnp.float32)
    slot_count = slotv.shape[1]
    slots = spread(slotv[...].astype(jnp.float32), (slot_count,) * 2, iota((slot_count,) * 2, 0))
    square = (rows, rows)
    ids_column = spread(ids, square, iota(square, 0))
    slot_of = jnp.sum(
        jnp.where(iota((slot_count, rows), 0).astype(jnp.float32) == ids, slots, 0.0),
        axis=0, keepdims=True,
    )
    earlier = (ids_column == ids) & (iota(square, 0) < iota(square, 1))
    target = slot_of * CAP + jnp.sum(jnp.where(earlier, 1.0, 0.0), axis=0, keepdims=True)
    target_column = spread(target, square, iota(square, 0))
    all_rows = jnp.sum(
        jnp.where(iota((rows, n), 0) == rem(iota((rows, n), 1), rows), target_column, 0.0),
        axis=0, keepdims=True,
    ).astype(jnp.int32) + (groups * LANES) * (div(iota((1, n), 1), rows))
    all_column = spread(target, (n, rows), rem(iota((n, rows), 0), rows)).astype(jnp.int32)
    head = div(iota((n, 128), 0), rows)
    place = jnp.broadcast_to(all_column, (n, 128))
    gsel[...] = div(place, LANES)
    lsel[...] = rem(div(place, CAP), SLOTS) * small + head * CAP + rem(place, CAP)
    wide = groups * strip

    def lane_code(i):
        lane = rem(div(i, small), SLOTS) * CAP + rem(i, CAP)
        return owner(div(i, strip)) * LANES + lane + groups * LANES * rem(div(i, CAP), size)

    sel[...] = jnp.where(lane_code(iota((wide, n), 0)) == all_rows, 1.0, 0.0).astype(jnp.bfloat16)
    back[...] = jnp.where(
        lane_code(iota((n, wide), 1)) == all_column + (groups * LANES) * div(iota((n, 1), 0), rows),
        1.0, 0.0,
    ).astype(jnp.bfloat16)
    box = (size * half, half * suf)
    for h in range(2):
        limit = spread(lengths, (size * half, rows), rem(iota((size * half, rows), 0), half) + h * half)
        kept = (div(iota(box, 1), suf) == rem(iota(box, 0), half)) & (
            rem(iota(box, 1), suf) + tp * suf < limit.astype(jnp.int32)
        )
        bias[h] = jnp.where(kept, 0.0, MASKED)

    o_copy().wait_recv()
    each(0, zs - 1, lambda i: w_copy(outward(i, zs)).start())
    each(1, zs, lambda d: a_copy(d).wait_recv())
    for d in beside:
        b_copy(d).start()

    def block_of(d):
        return rem(y - d + ys, ys)

    def c_copy(d, e):
        yy = block_of(d)
        return remote(
            xs.at[yy, e], xr.at[yy, e], c_send.at[d, e], c_recv.at[d, e], (owner(e), tp)
        )

    def c_stage(d):
        yy = block_of(d)
        for kk in range(ky):
            part = slice(kk * strip, (kk + 1) * strip)
            block = qall[pl.ds((yy * ky + kk) * dk, dk)].reshape(n, HD)
            picked = mm(sel[...], block).astype(jnp.bfloat16).reshape(groups, strip, HD)
            xs[yy, :, part, :] = picked
            xr[yy, 0, part, :] = picked[0]

    def f_copy(e, d):
        return remote(
            xr.at[y, e], xr.at[y, e], f_send.at[e - NEAR, d], f_recv.at[e - NEAR, d], y_peer(d)
        )

    def suffix(k):
        lanes = pl.ds(pl.multiple_of(k * HD, HD), HD)
        block = qall[pl.ds(k * dk, dk)].reshape(size, rows, HD)
        for h in range(2):
            part = slice(h * half, (h + 1) * half)
            at = slice(h * half * suf, (h + 1) * half * suf)
            asking = block[:, part, :].reshape(size * half, HD)
            value, level = attend(nt(asking, sk[0, at, lanes]) + bias[h], sk[1, at, lanes])
            so[k, :, part, :] = value.reshape(size, half, HD)
            sl[k, :, part, :] = jnp.broadcast_to(level, (size * half, 128)).reshape(size, half, 128)

    def suffixes(d):
        yy = block_of(d)
        for kk in range(ky):
            suffix(yy * ky + kk)

    c_stage(0)
    each(1, groups, lambda e: c_copy(0, groups - e).start())
    loads[4].wait()
    suffixes(0)

    def ask(d):
        if d == opposite:
            each(1, zs, lambda i: w_copy(i).wait_recv())
        else:
            b_copy(d).wait_recv()
        c_stage(d)
        each(1, NEAR, lambda e: c_copy(d, e).start())
        suffixes(d)

    def pass_on(e):
        c_copy(0, e).wait_recv()
        each(1, ys, lambda d: f_copy(e, d).start())

    order = [opposite] + beside
    ask(order[0])
    each(NEAR, groups, pass_on)

    loads[5].wait()

    def e_copy(d, e):
        yy = block_of(d)
        return remote(
            po.at[yy, e], pr.at[yy, e], e_send.at[d, e], e_recv.at[d, e], (asker(e), tp)
        )

    def el_copy(d, e):
        yy = block_of(d)
        return remote(
            ls.at[yy, e], lr.at[yy, e], el_send.at[d, e], el_recv.at[d, e], (asker(e), tp)
        )

    def r_copy(e, d):
        i = e - NEAR
        return remote(
            po.at[block_of(d), e], fr.at[d, i], r_send.at[i, d], r_recv.at[i, d], y_back(d)
        )

    def rl_copy(e, d):
        i = e - NEAR
        return remote(
            ls.at[block_of(d), e], flr.at[d, i], rl_send.at[i, d], rl_recv.at[i, d], y_back(d)
        )

    def m_copy(e):
        i = e - NEAR
        return remote(fo.at[i], pr.at[y, e], m_send.at[i], m_recv.at[i], (asker(e), tp))

    def ml_copy(e):
        i = e - NEAR
        return remote(fl.at[i], lr.at[y, e], ml_send.at[i], ml_recv.at[i], (asker(e), tp))

    def prefix(d):
        yy = block_of(d)
        each(1, NEAR, lambda e: c_copy(d, e).wait_recv())
        for kk in range(ky):
            lanes = pl.ds(pl.multiple_of((yy * ky + kk) * HD, HD), HD)
            for j in range(SLOTS):
                part = slice(kk * strip + j * small, kk * strip + (j + 1) * small)
                asking = xr[yy, :, part, :].reshape(groups * small, HD)
                value, level = attend(nt(asking, pk[0, j, :, lanes]), pk[1, j, :, lanes])
                value = value.astype(jnp.bfloat16).reshape(groups, small, HD)
                po[yy, :, part, :] = value
                pr[yy, 0, part, :] = value[0]
                lc[:, part, :] = jnp.broadcast_to(level, (groups * small, 128)).reshape(
                    groups, small, 128
                )

        for e in range(groups):
            ls[yy, e] = to_row(lc[e], lane_rows)
        lr[yy, 0] = ls[yy, 0]

        def send(e):
            e_copy(d, e).start()
            el_copy(d, e).start()

        each(1, NEAR, send)

    for d in order[1:]:
        ask(d)
    prefix(0)

    def prefix_step(i):
        d = outward(i - 1, ys)
        each(NEAR, groups, lambda e: f_copy(e, d).wait_recv())
        prefix(d)

        def send(e):
            r_copy(e, d).start()
            rl_copy(e, d).start()

        each(NEAR, groups, send)

    each(1, ys, prefix_step)

    def far_merge(e):
        i = e - NEAR

        def arrived(d):
            r_copy(e, d).wait_recv()
            rl_copy(e, d).wait_recv()

        each(1, ys, arrived)
        parts = [(po[y, e].astype(jnp.float32), to_column(ls[y, e, 0:1, :], lane_rows))]
        for d in range(1, ys):
            parts.append((fr[d, i].astype(jnp.float32), to_column(flr[d, i, 0:1, :], lane_rows)))
        value, level = merge(parts)
        fo[i] = value.astype(jnp.bfloat16)
        fl[i] = to_row(level, lane_rows)
        m_copy(e).start()
        ml_copy(e).start()

    def y_copy(d):
        return remote(yb.at[block_of(d)], yr.at[d], y_send.at[d], y_recv.at[d], y_back(d))

    def yl_copy(d):
        return remote(yl.at[block_of(d)], ylr.at[d], yl_send.at[d], yl_recv.at[d], y_back(d))

    def join(d, owners):
        yy = block_of(d)

        def arrived(e):
            e_copy(d, e).wait_recv()
            el_copy(d, e).wait_recv()

        each(1, NEAR, arrived)
        levels = jnp.full((n, 128), MASKED, jnp.float32)
        for e in range(owners):
            levels = jnp.where(gsel[...] == owner(e), lr[yy, e, 0:1, :], levels)
        for kk in range(ky):
            hit = iota((n, 128), 1) == lsel[...] + kk * strip
            level = jnp.sum(jnp.where(hit, levels, 0.0), axis=1, keepdims=True)
            parts = pr[yy, 0:owners, kk * strip : (kk + 1) * strip, :].reshape(owners * strip, HD)
            k = yy * ky + kk
            value, joint = merge(
                [
                    (mm(back[:, 0 : owners * strip], parts), level),
                    (so[k].reshape(n, HD), sl[k].reshape(n, 128)[:, 0:1]),
                ]
            )
            yb[yy, kk * dk : (kk + 1) * dk] = value.astype(jnp.bfloat16).reshape(dk, OWN * rows, HD)
            for i in range(dk // 2):
                row = to_row(joint[i * 128 : (i + 1) * 128], 128)
                yl[yy, kk * dk // 2 + i] = row

    across = rem(y + opposite, ys)

    def u_copy(d):
        return remote(yb.at[across, rem(z + d, zs)], ur.at[d], u_send.at[d], u_recv.at[d], z_peer(d))

    def ul_copy(d):
        return remote(
            yl.at[across, div(rem(z + d, zs), 2)], ulr.at[d], ul_send.at[d], ul_recv.at[d], z_peer(d)
        )

    def v_copy():
        return remote(vb, vr, v_send.at[0], v_recv.at[0], y_peer(opposite))

    def vl_copy():
        return remote(vl, vlr, v_send.at[1], v_recv.at[1], y_peer(opposite))

    def u_start(i):
        d = outward(i, zs)
        u_copy(d).start()
        ul_copy(d).start()

    join(opposite, NEAR)
    each(0, zs - 1, u_start)
    for d in beside:
        join(d, NEAR)
        y_copy(d).start()
        yl_copy(d).start()
    each(NEAR, groups, far_merge)

    def far_arrived(e):
        m_copy(e).wait_recv()
        ml_copy(e).wait_recv()

    each(NEAR, groups, far_arrived)
    join(0, groups)

    def u_arrived(d):
        u_copy(d).wait_recv()
        ul_copy(d).wait_recv()

    each(1, zs, u_arrived)
    shift = rem(z, 2) * 64
    parts = [(yb[across, z].astype(jnp.float32), to_column(yl[across, div(z, 2), 0:1, :], 64, shift))]
    for d in range(1, zs):
        parts.append((ur[d].astype(jnp.float32), to_column(ulr[d, 0:1, :], 64, shift)))
    value, level = merge(parts)
    vb[...] = value.astype(jnp.bfloat16)
    vl[...] = to_row(level, 64)
    v_copy().start()
    vl_copy().start()

    def y_arrived(d):
        y_copy(d).wait_recv()
        yl_copy(d).wait_recv()

    for d in beside:
        y_arrived(d)

    def y_merge(i):
        pair = pl.ds(i * 2, 2)
        parts = [(yb[y, pair].reshape(128, HD).astype(jnp.float32), to_column(yl[y, i, 0:1, :], 128))]
        for d in beside:
            value = yr[d, pair].reshape(128, HD).astype(jnp.float32)
            parts.append((value, to_column(ylr[d, i, 0:1, :], 128)))
        value, level = merge(parts)
        zb[pair] = value.astype(jnp.bfloat16).reshape(2, 64, HD)
        zl[pair] = jnp.broadcast_to(to_row(level, 128)[None], (2, 1, 128))

    each(0, zs // 2, y_merge)

    def z_copy(d):
        return remote(zb.at[rem(z + d, zs)], zr.at[d], z_send.at[d], z_recv.at[d], z_peer(d))

    def zl_copy(d):
        return remote(zl.at[rem(z + d, zs)], zlr.at[d], zl_send.at[d], zl_recv.at[d], z_peer(d))

    def z_start(d):
        z_copy(d).start()
        zl_copy(d).start()

    each(0, zs - 1, lambda i: z_start(outward(i, zs)))

    def z_arrived(d):
        z_copy(d).wait_recv()
        zl_copy(d).wait_recv()

    each(1, zs, z_arrived)
    v_copy().wait_recv()
    vl_copy().wait_recv()
    parts = [
        (zb[z].astype(jnp.float32), to_column(zl[z, 0:1, :], 64, shift)),
        (vr[...].astype(jnp.float32), to_column(vlr[0:1, :], 64)),
    ]
    for d in range(1, zs):
        parts.append((zr[d].astype(jnp.float32), to_column(zlr[d, 0:1, :], 64, shift)))
    attended = merge(parts)[0].astype(jnp.bfloat16)
    attended = jnp.concatenate([attended[0:rows], attended[rows : 2 * rows]], axis=1)

    loads[6].wait()

    def z_order(i):
        return rem(outward(i, zs), zs)

    span = zs // 2

    def wy_copy(h, d):
        part = pl.ds(h * span, span)
        return remote(
            wp.at[block_of(d), part], wr.at[d, part], wy_send.at[h, d], wy_recv.at[h, d], y_back(d)
        )

    def wu_copy(i):
        return remote(
            wp.at[across, i], wur.at[i], wu_send.at[i], wu_recv.at[i], z_peer(z_order(i))
        )

    def wv_copy():
        return remote(wvb, wvr, wv_send.at[0], wv_recv.at[0], y_peer(opposite))

    def wz_copy(i):
        return remote(wz.at[i], wzr.at[i], wz_send.at[i], wz_recv.at[i], z_peer(z_order(i)))

    def project(h, d):
        yy = block_of(d)
        for i in range(h * span, (h + 1) * span):
            columns = (yy * zs + rem(z + z_order(i), zs)) * (OWN * HD)
            columns = pl.ds(pl.multiple_of(columns, OWN * HD), OWN * HD)
            wp[yy, i] = mm(attended, wv[:, columns]).astype(jnp.bfloat16)

    for h in range(2):
        project(h, opposite)
        each(h * span, min((h + 1) * span, zs - 1), lambda i: wu_copy(i).start())
        for d in beside:
            project(h, d)
            wy_copy(h, d).start()
    project(0, 0)
    project(1, 0)
    def y_sum(i):
        total = wp[y, i].astype(jnp.float32)
        for d in beside:
            total += wr[d, i].astype(jnp.float32)
        return total

    def w_step(i):
        wz[i] = y_sum(i).astype(jnp.bfloat16)
        wz_copy(i).start()

    def z_sent(d):
        a_copy(d).wait_send()
        z_copy(d).wait_send()
        zl_copy(d).wait_send()
        w_copy(d).wait_send()
        u_copy(d).wait_send()
        ul_copy(d).wait_send()

    each(1, zs, z_sent)

    for d in beside:
        b_copy(d).wait_send()
        y_copy(d).wait_send()
        yl_copy(d).wait_send()
    o_copy().wait_send()
    v_copy().wait_send()
    vl_copy().wait_send()

    def near_sent(d):
        def one(e):
            c_copy(d, e).wait_send()
            e_copy(d, e).wait_send()
            el_copy(d, e).wait_send()

        each(1, NEAR, one)

    def far_sent(e):
        def one(d):
            f_copy(e, d).wait_send()
            r_copy(e, d).wait_send()
            rl_copy(e, d).wait_send()

        c_copy(0, e).wait_send()
        each(1, ys, one)
        m_copy(e).wait_send()
        ml_copy(e).wait_send()

    each(0, ys, near_sent)
    each(NEAR, groups, far_sent)

    for d in beside:
        wy_copy(0, d).wait_recv()
    each(0, span, w_step)
    each(0, zs - 1, lambda i: wu_copy(i).wait_recv())
    total = wp[across, zs - 1].astype(jnp.float32)
    for i in range(zs - 1):
        total += wur[i].astype(jnp.float32)
    wvb[...] = total.astype(jnp.bfloat16)
    wv_copy().start()
    for d in beside:
        wy_copy(1, d).wait_recv()
    each(span, zs - 1, w_step)
    total = y_sum(zs - 1)
    wv_copy().wait_recv()
    total += wvr[...].astype(jnp.float32)
    each(0, zs - 1, lambda i: wz_copy(i).wait_recv())
    for i in range(zs - 1):
        total += wzr[i].astype(jnp.float32)
    out_ref[...] = total.astype(jnp.bfloat16)

    def last_sent(i):
        wu_copy(i).wait_send()
        wz_copy(i).wait_send()

    each(0, zs - 1, last_sent)
    for d in beside:
        wy_copy(0, d).wait_send()
        wy_copy(1, d).wait_send()
    wv_copy().wait_send()


def body(zs, queries, prefix_ids, suffix_lengths, owner_slots, prefix_cache, suffix_cache, wo):
    groups = lax.axis_size("grp")
    shards = lax.axis_size("tp")
    ys = shards // zs
    rows = queries.shape[0]
    suf = suffix_cache.shape[2]
    kvh = prefix_cache.shape[3] // HD
    size = shards * OWN // kvh
    n = size * rows
    ky = kvh // ys
    strip = SLOTS * size * CAP
    lane_rows = ky * strip
    far = groups - NEAR

    dims = (groups, ys, zs, kvh, rows, suf)
    bf, f32 = jnp.bfloat16, jnp.float32
    dma = pltpu.SemaphoreType.DMA
    vmem = pl.BlockSpec(memory_space=pltpu.VMEM)
    hbm = pl.BlockSpec(memory_space=pltpu.HBM)
    V = pltpu.VMEM
    scratch = [
        V(queries.shape, bf),
        V((1, rows), jnp.int32),
        V((1, rows), jnp.int32),
        V((1, owner_slots.shape[0]), jnp.int32),
        V(prefix_cache.shape, bf),
        V((2, rows * suf, kvh * HD), bf),
        V(wo.shape, bf),
        V((shards, OWN * rows, HD), bf),
        V((ys, groups, lane_rows, HD), bf),
        V((ys, groups, lane_rows, HD), bf),
        V((ys, groups, lane_rows, HD), bf),
        V((ys, groups, lane_rows, HD), bf),
        V((ys, groups, 1, 128), f32),
        V((ys, groups, 1, 128), f32),
        V((ys, far, lane_rows, HD), bf),
        V((ys, far, 1, 128), f32),
        V((far, lane_rows, HD), bf),
        V((far, 1, 128), f32),
        V((groups, lane_rows, 128), f32),
        V((kvh, size, rows, HD), f32),
        V((kvh, size, rows, 128), f32),
        V((groups * strip, n), bf),
        V((n, groups * strip), bf),
        V((n, 128), jnp.int32),
        V((n, 128), jnp.int32),
        V((2, n // 2, rows * suf // 2), f32),
        V((ys, zs, OWN * rows, HD), bf),
        V((ys, zs // 2, 1, 128), f32),
        V((ys, zs, OWN * rows, HD), bf),
        V((ys, zs // 2, 1, 128), f32),
        V((zs, OWN * rows, HD), bf),
        V((zs, 1, 128), f32),
        V((OWN * rows, HD), bf),
        V((1, 128), f32),
        V((OWN * rows, HD), bf),
        V((1, 128), f32),
        V((zs, OWN * rows, HD), bf),
        V((zs, 1, 128), f32),
        V((zs, OWN * rows, HD), bf),
        V((zs, 1, 128), f32),
        V((ys, zs, rows, OWN * HD), bf),
        V((ys, zs, rows, OWN * HD), bf),
        V((zs, rows, OWN * HD), bf),
        V((zs, rows, OWN * HD), bf),
        V((zs, rows, OWN * HD), bf),
        V((rows, OWN * HD), bf),
        V((rows, OWN * HD), bf),
        dma((7,)),
        dma((zs,)), dma((zs,)),
        dma((ys,)), dma((ys,)),
        dma((1,)), dma((1,)),
        dma((zs,)), dma((zs,)),
        dma((ys, groups)), dma((ys, groups)),
        dma((far, ys)), dma((far, ys)),
        dma((ys, groups)), dma((ys, groups)),
        dma((ys, groups)), dma((ys, groups)),
        dma((far, ys)), dma((far, ys)),
        dma((far, ys)), dma((far, ys)),
        dma((far,)), dma((far,)),
        dma((far,)), dma((far,)),
        dma((ys,)), dma((ys,)), dma((ys,)), dma((ys,)),
        dma((zs,)), dma((zs,)), dma((zs,)), dma((zs,)),
        dma((zs,)), dma((zs,)), dma((zs,)), dma((zs,)),
        dma((2,)), dma((2,)),
        dma((zs,)), dma((zs,)),
        dma((1,)), dma((1,)),
        dma((2, ys)), dma((2, ys)),
        dma((zs,)), dma((zs,)),
    ]
    return pl.pallas_call(
        functools.partial(kernel, dims),
        out_shape=jax.ShapeDtypeStruct((rows, wo.shape[1] // shards), bf),
        in_specs=[hbm] * 7,
        out_specs=vmem,
        scratch_shapes=scratch,
        compiler_params=pltpu.CompilerParams(
            collective_id=0, has_side_effects=True, vmem_limit_bytes=62 * 1024 * 1024
        ),
        name="decode_attention",
    )(
        queries, prefix_ids.reshape(1, rows), suffix_lengths.reshape(1, rows),
        owner_slots.reshape(1, -1), prefix_cache,
        suffix_cache.reshape(2, rows * suf, kvh * HD), wo,
    )


def solution(mesh, zs=Z_SIZE):
    placed = (
        P("grp", "tp"),
        P("grp", None),
        P("grp"),
        P(),
        P(None, "grp", "tp", None),
        P(None, "grp", "tp", None),
        P("tp", None),
    )
    return jax.shard_map(
        functools.partial(body, zs),
        mesh=mesh, in_specs=placed, out_specs=P("grp", "tp"), check_vma=False,
    )
```
